512 devices in a mesh: context: 64 (over y, z), tensor: 8 (over x, core).
Axes of the slice: x: 4, y: 4, z: 16, core: 2. Of those that a mesh axis runs over, the one named last changes fastest.
Arguments:
- tokens: bfloat16 [8192, 8192], P('context', 'tensor'), may hold values from -6 to 6
- grad_out: bfloat16 [8192, 8192], P('context', 'tensor'), may hold values from -6 to 6
- keep_count: int32 [64], P('context'), may hold values from 1 to 6, as said below
- keep_pos: int32 [64, 6], P('context'), may hold values from 0 to 127, as said below
- router: bfloat16 [64, 6], P('context'), may hold values from 0.19921875 to 1
- gate_weight: bfloat16 [16384, 8192], P(('tensor', 'context')), may hold values from -0.25 to 0.25
- up_weight: bfloat16 [16384, 8192], P(('tensor', 'context')), may hold values from -0.25 to 0.25
- down_weight: bfloat16 [16384, 8192], P(('tensor', 'context')), may hold values from -0.046875 to 0.046875
Outputs:
- grad_tokens: bfloat16 [8192, 8192], P('context', 'tensor')
- grad_gate: bfloat16 [16384, 8192], P(('tensor', 'context'))
- grad_up: bfloat16 [16384, 8192], P(('tensor', 'context'))
- grad_down: bfloat16 [16384, 8192], P(('tensor', 'context'))
- kept_grad: float32 [128, 8192], P(None, 'tensor')
The draws below stay inside these ranges and needn't reach their ends.
Inputs may be any that keep to these rules, and one draw needn't show every extreme that they name: keep_count sums to 128; the first 12 shards keep exactly 6 rows each, every other shard keeps 1 to 5 rows. `keep_pos`: the 6 positions in one row are distinct; only the first keep_count[c] of row c are used.
All inputs are finite; a program needn't handle non-finite values.
Results may differ from the reference program's by a relative error of at most 0.009.
Values may be sent and summed in bfloat16 or wider, within the bound.
No kernel may reach another device: no remote copies, remote signals or barrier semaphores. Data moves between devices by JAX's collectives and lax.ppermute only.
A program may use at most 128 MiB of HBM per device.

```python
import jax
import jax.numpy as jnp

D = 8192
FF = 16384
TOK_DEV = 128
CAP = 2
KMAX = 6
KEEP = 128
TOKENS = 8192
N_CONTEXT = 64


def shard_positions(key):
    return jax.random.permutation(key, TOK_DEV)[:KMAX].astype(jnp.int32)


def draw_keep_count(key, part):
    key = jax.random.fold_in(key, 23)
    heavy = N_CONTEXT // 5
    light = N_CONTEXT - heavy
    extras = KEEP - KMAX * heavy - light
    picks = jax.random.randint(key, (extras,), 0, light).astype(jnp.int32)
    hits = (picks[:, None] == jnp.arange(light, dtype=jnp.int32)[None, :]).astype(jnp.int32)
    tail = (1 + jnp.sum(hits, axis=0)).astype(jnp.int32)
    head = jnp.full((heavy,), KMAX, jnp.int32)
    return jnp.concatenate([head, tail]).astype(jnp.int32)


def draw_keep_pos(key, part):
    key = jax.random.fold_in(key, 11)
    shard_keys = jax.random.split(key, N_CONTEXT)
    rows = jax.vmap(shard_positions)(shard_keys)
    middle = (jax.random.permutation(jax.random.fold_in(key, 5), TOK_DEV - 2)[:KMAX - 2] + 1).astype(jnp.int32)
    first = jnp.concatenate([jnp.array([0, TOK_DEV - 1], jnp.int32), middle])
    return rows.at[0].set(first).astype(jnp.int32)


def spiked(entries, rng, source, target, blocks, factor):
    def block_of(dim):
        return (jnp.arange(entries.shape[dim]) // (entries.shape[dim] // blocks)).reshape((-1,) + (1,) * (entries.ndim - 1 - dim))

    first = jax.random.permutation(rng, blocks)[block_of(target)]
    other_side = (block_of(target) + blocks // 2) % blocks
    return jnp.where((block_of(source) == first) | (block_of(source) == other_side), factor * entries, entries)


def shard_levels(own_key, shape, cuts, low, largest):
    gain = 1.0
    for dim, blocks in cuts:
        heights = jax.random.uniform(jax.random.fold_in(jax.random.fold_in(own_key, 6), dim), (blocks,), jnp.float32, low / len(cuts), largest / len(cuts))
        gain = gain * jnp.repeat(jnp.exp(heights), shape[dim] // blocks).reshape((-1,) + (1,) * (len(shape) - 1 - dim))
    return gain


def gaussian(own_key, shape, spread, limit, cuts=(), kind=jnp.bfloat16):
    result = jax.random.normal(own_key, shape, jnp.float32) * spread
    if len(cuts) > 0:
        result = shard_levels(own_key, shape, cuts, -0.22, 0.18) * result
    return jnp.clip(result, min=-limit, max=limit).astype(kind)


def gaussian_with(own_key, dims, spread, bound, shards, heavy, held_as=jnp.bfloat16):
    values = spread * jax.random.normal(own_key, dims, jnp.float32)
    if shards:
        values = values * shard_levels(own_key, dims, shards, -0.22, 0.18)
    return jnp.clip(spiked(values, jax.random.fold_in(own_key, 3), *heavy), -bound, bound).astype(held_as)


def setup_inputs(seed: int = 0) -> dict:
    seeds = jax.random.split(jax.random.key(seed), 9)
    tokens = gaussian(seeds[0], (TOKENS, D), 1.0, 6.0, ((0, 64), (1, 8)))
    grad_out = gaussian(seeds[1], (TOKENS, D), 1.0, 6.0, ((0, 64), (1, 8)))
    keep_count = draw_keep_count(jax.random.fold_in(seeds[8], 71), 0)
    keep_pos = draw_keep_pos(jax.random.fold_in(seeds[8], 71), 0)
    router = jnp.clip(0.19921875 + 0.80078125 * jax.random.uniform(seeds[4], (N_CONTEXT, KMAX), jnp.float32) ** shard_levels(seeds[4], (N_CONTEXT, KMAX), ((0, 64),), -0.2, 0.2), 0.19921875, 1.0).astype(jnp.bfloat16)
    gate_weight = gaussian_with(seeds[5], (FF, D), D ** -0.5, 0.25, ((0, 512),), (0, 1, 512, 6.0))
    up_weight = gaussian_with(seeds[6], (FF, D), D ** -0.5, 0.25, ((0, 512),), (0, 1, 512, 6.0))
    down_weight = gaussian(seeds[7], (FF, D), FF ** -0.5, 0.046875, ((0, 512),))
    return {"tokens": tokens, "grad_out": grad_out, "keep_count": keep_count, "keep_pos": keep_pos, "router": router, "gate_weight": gate_weight, "up_weight": up_weight, "down_weight": down_weight}


def reference(tokens, grad_out, keep_count, keep_pos, router, gate_weight, up_weight, down_weight):
    shard_count = keep_count.shape[0]
    most_rows = keep_pos.shape[1]
    kept_total = CAP * shard_count
    counts = keep_count.astype(jnp.int32)
    starts = (jnp.cumsum(counts) - counts).astype(jnp.int32)
    column_ids = jnp.arange(most_rows, dtype=jnp.int32)
    live_rows = column_ids[None, :] < counts[:, None]
    slot_ids = jnp.where(live_rows, starts[:, None] + column_ids[None, :], kept_total).astype(jnp.int32)
    token_ids = (jnp.arange(shard_count, dtype=jnp.int32)[:, None] * TOK_DEV + keep_pos.astype(jnp.int32)).astype(jnp.int32)
    source = jnp.zeros((kept_total + 1,), jnp.int32).at[slot_ids.reshape(-1)].set(token_ids.reshape(-1))[:kept_total]
    row_weight = jnp.zeros((kept_total + 1,), jnp.float32).at[slot_ids.reshape(-1)].set(router.reshape(-1).astype(jnp.float32))[:kept_total]
    kept_x = jnp.take(tokens, source, axis=0)
    kept_dy = jnp.take(grad_out, source, axis=0)
    gate_pre = jnp.dot(kept_x, gate_weight.T, preferred_element_type=jnp.float32)
    up_pre = jnp.dot(kept_x, up_weight.T, preferred_element_type=jnp.float32)
    sigmoid_gate = jax.nn.sigmoid(gate_pre)
    activated = gate_pre * sigmoid_gate
    hidden = (activated * up_pre).astype(jnp.bfloat16)
    back_proj = jnp.dot(kept_dy, down_weight.T, preferred_element_type=jnp.float32)
    hidden_grad = row_weight[:, None] * back_proj
    gate_grad = (hidden_grad * sigmoid_gate * (1.0 + gate_pre * (1.0 - sigmoid_gate)) * up_pre).astype(jnp.bfloat16)
    up_grad = (hidden_grad * activated).astype(jnp.bfloat16)
    scaled_dy = (row_weight[:, None] * kept_dy.astype(jnp.float32)).astype(jnp.bfloat16)
    grad_down = jnp.dot(hidden.T, scaled_dy, preferred_element_type=jnp.float32).astype(jnp.bfloat16)
    grad_gate = jnp.dot(gate_grad.T, kept_x, preferred_element_type=jnp.float32).astype(jnp.bfloat16)
    grad_up = jnp.dot(up_grad.T, kept_x, preferred_element_type=jnp.float32).astype(jnp.bfloat16)
    kept_grad = jnp.dot(gate_grad, gate_weight, preferred_element_type=jnp.float32) + jnp.dot(up_grad, up_weight, preferred_element_type=jnp.float32)
    grad_tokens = grad_out.astype(jnp.float32).at[source].add(kept_grad).astype(jnp.bfloat16)
    return grad_tokens, grad_gate, grad_up, grad_down, kept_grad
```

```python
import jax
import jax.numpy as jnp
from jax import lax
from jax.sharding import Mesh, PartitionSpec as P

NY, NZ, NX, NC = 4, 16, 4, 2
HEAVY = 12
MOST = 6
PLANE = 35
KEPT = 128
BF = jnp.bfloat16
F32 = jnp.float32


def one_hot_rows(hot, rows):
    return jnp.dot(hot.astype(BF), rows, preferred_element_type=F32).astype(BF)


def spread(piece, axes, n):
    return lax.all_to_all(
        jnp.broadcast_to(piece[None], (n,) + piece.shape), axes, 0, 0, tiled=True
    )


def body(tokens, grad_out, keep_count, keep_pos, router, gate_weight, up_weight, down_weight):
    tok_dev, width = tokens.shape
    yi, zi, ci = lax.axis_index("y"), lax.axis_index("z"), lax.axis_index("core")
    shard = yi * NZ + zi

    j8 = jnp.arange(8, dtype=jnp.int32)
    live = j8 < keep_count[0]
    pos8 = jnp.pad(keep_pos[0], (0, 8 - MOST))
    picker = (pos8[:, None] == jnp.arange(tok_dev)[None, :]) & live[:, None]
    lane = jnp.arange(128)[None, :]
    weight8 = jnp.pad(router[0], (0, 8 - MOST)).astype(F32)[:, None]
    meta = jnp.where(lane == 0, weight8, 0.0)
    meta = jnp.where(lane == 1, 1.0, meta)
    meta = jnp.where(lane == 2, shard.astype(F32), meta)
    meta = jnp.where(lane == 3, j8.astype(F32)[:, None], meta)
    meta = jnp.where(live[:, None], meta, 0.0).astype(BF)
    x_rows = jnp.concatenate([one_hot_rows(picker, tokens), meta], axis=1)
    dy_rows = jnp.concatenate([one_hot_rows(picker, grad_out), meta], axis=1)
    column = spread(jnp.concatenate([x_rows, dy_rows], axis=0), "y", NY)

    column = column.reshape(NY, 2, 8, width + 128)
    q = jnp.arange(32)
    qy, qj = q // 8, q % 8
    col_valid = column[:, 0, :, width + 1].reshape(32) > 0.5
    steady = jnp.where(
        zi < HEAVY,
        jnp.where(qy == 0, jnp.where(qj < MOST, qj, 99), jnp.where(qj == 0, 5 + qy, 99)),
        jnp.where(qj == 0, qy, 99),
    )
    extra = col_valid & (qj >= 1) & ((qy > 0) | (zi >= HEAVY))
    nth = jnp.sum((q[None, :] < q[:, None]) & extra[None, :], axis=1)
    p4 = jnp.arange(4)[:, None]
    hot = jnp.where(
        p4 < 3,
        steady[None, :] == 4 * p4 + ((yi - zi) % 4),
        extra[None, :] & (nth[None, :] == yi),
    )
    picked = jnp.concatenate(
        [
            one_hot_rows(hot, column[:, 0].reshape(32, width + 128)),
            one_hot_rows(hot, column[:, 1].reshape(32, width + 128)),
        ],
        axis=0,
    )
    plane = spread(picked, "z", NZ).reshape(NZ, 2, 4, width + 128)

    p_valid = plane[:, 0, :, width + 1].reshape(64) > 0.5
    i64 = jnp.arange(64)
    rank = jnp.sum((i64[None, :] < i64[:, None]) & p_valid[None, :], axis=1)
    hot = (rank[None, :] == jnp.arange(PLANE)[:, None]) & p_valid[None, :]
    px = plane[:, 0].reshape(64, width + 128)
    pd = plane[:, 1].reshape(64, width + 128)
    facts = jnp.einsum(
        "mv,tm->vt", px[:, width : width + 4], hot.astype(BF), preferred_element_type=F32
    ).astype(BF)
    facts = jnp.pad(facts, ((0, 0), (0, 128 - PLANE))).reshape(1, 512)
    packed = jnp.concatenate(
        [
            one_hot_rows(hot, px[:, :width]),
            one_hot_rows(hot, pd[:, :width]),
            jnp.pad(facts, ((0, 1), (0, width - 512))),
        ],
        axis=0,
    )
    everything = spread(packed, ("y", "x"), NY * NX).reshape(NY, NX, 2 * PLANE + 2, width)

    facts = everything[:, 0, 2 * PLANE, :512].reshape(NY, 4, 128)[:, :, :PLANE].astype(F32)
    facts = facts.transpose(1, 0, 2).reshape(4, NY * PLANE)
    valid = facts[1] > 0.5
    key = facts[2] * 8 + facts[3]
    slot = jnp.sum((key[None, :] < key[:, None]) & valid[None, :], axis=1)
    hot = (slot[None, :] == jnp.arange(KEPT)[:, None]) & valid[None, :]
    row_scale = jnp.sum(jnp.where(hot, facts[0][None, :], 0.0), axis=1, keepdims=True)
    start_here = jnp.sum((valid & (facts[2] < shard.astype(F32))).astype(jnp.int32))

    def ordered(part):
        part = part.transpose(0, 2, 1, 3).reshape(NY * PLANE, NX * width)
        return one_hot_rows(hot, part)

    own = jnp.stack(
        [ordered(everything[:, :, :PLANE]), ordered(everything[:, :, PLANE : 2 * PLANE])]
    ).reshape(2, KEPT, NX, 1, width)
    other = lax.ppermute(own, "core", [(0, 1), (1, 0)])
    kept = jnp.concatenate(
        [jnp.where(ci == 0, own, other), jnp.where(ci == 0, other, own)], axis=3
    ).reshape(2, KEPT, NX * NC * width)
    kept_x, kept_dy = kept[0], kept[1]

    gate_pre = jnp.einsum("kd,fd->kf", kept_x, gate_weight, preferred_element_type=F32)
    up_pre = jnp.einsum("kd,fd->kf", kept_x, up_weight, preferred_element_type=F32)
    sigmoid_gate = jax.nn.sigmoid(gate_pre)
    activated = gate_pre * sigmoid_gate
    hidden = (activated * up_pre).astype(BF)
    back_proj = jnp.einsum("kd,fd->kf", kept_dy, down_weight, preferred_element_type=F32)
    hidden_grad = row_scale * back_proj
    gate_grad = (
        hidden_grad * sigmoid_gate * (1.0 + gate_pre * (1.0 - sigmoid_gate)) * up_pre
    ).astype(BF)
    up_grad = (hidden_grad * activated).astype(BF)
    scaled_dy = (row_scale * kept_dy.astype(F32)).astype(BF)

    partial = jnp.einsum("kf,fd->kd", gate_grad, gate_weight, preferred_element_type=F32)
    partial = partial + jnp.einsum("kf,fd->kd", up_grad, up_weight, preferred_element_type=F32)
    partial = partial.reshape(KEPT, NX, NC, width)
    mine = lax.dynamic_index_in_dim(partial, ci, 2, keepdims=False)
    theirs = lax.dynamic_index_in_dim(partial, 1 - ci, 2, keepdims=False).astype(BF)
    came = lax.ppermute(theirs, "core", [(0, 1), (1, 0)])

    grad_down = jnp.einsum("kf,kd->fd", hidden, scaled_dy, preferred_element_type=F32).astype(BF)
    grad_gate = jnp.einsum("kf,kd->fd", gate_grad, kept_x, preferred_element_type=F32).astype(BF)
    grad_up = jnp.einsum("kf,kd->fd", up_grad, kept_x, preferred_element_type=F32).astype(BF)

    chip = (mine + came.astype(F32)).astype(BF)
    chip = chip.reshape(NY, KEPT // NY, NX, width).transpose(0, 2, 1, 3)
    chip = chip.reshape(NY * NX, KEPT // NY, width)
    chip = lax.all_to_all(chip, ("y", "x"), 0, 0, tiled=True)
    quarter = jnp.sum(chip.astype(F32), axis=0).astype(BF)
    rows, cols = KEPT // NY // 4, width // 4
    quarter = quarter.reshape(4, rows, 4, cols).transpose(0, 2, 1, 3).reshape(NZ, rows, cols)
    quarter = lax.all_to_all(quarter, "z", 0, 0, tiled=True)
    block = jnp.sum(quarter.astype(F32), axis=0).astype(BF)
    quarter = spread(block, "z", NZ).reshape(4, 4, rows, cols).transpose(0, 2, 1, 3)
    summed = spread(quarter.reshape(KEPT // NY, width), "y", NY).reshape(KEPT, width)
    summed = summed.astype(F32)

    extended = jnp.concatenate([summed, jnp.zeros((8, width), F32)], axis=0)
    own_rows = lax.dynamic_slice_in_dim(extended, start_here, 8, 0)
    added = jnp.dot(
        picker.astype(F32).T,
        own_rows,
        precision=lax.Precision.HIGHEST,
        preferred_element_type=F32,
    )
    grad_tokens = (grad_out.astype(F32) + added).astype(BF)
    return (grad_tokens, grad_gate, grad_up, grad_down, summed)


def solution(mesh):
    grid = Mesh(mesh.devices.reshape(NY, NZ, NX, NC), ("y", "z", "x", "core"))
    context, tensor = ("y", "z"), ("x", "core")
    units = P(tensor + context, None)
    return jax.shard_map(
        body,
        mesh=grid,
        in_specs=(
            P(context, tensor),
            P(context, tensor),
            P(context),
            P(context, None),
            P(context, None),
            units,
            units,
            units,
        ),
        out_specs=(P(context, tensor), units, units, units, P(None, tensor)),
        check_vma=False,
    )
```

```python
import jax
import jax.numpy as jnp
from jax import lax
from jax.experimental import pallas as pl
from jax.experimental.pallas import tpu as pltpu
from jax.sharding import Mesh, PartitionSpec as P

NY, NZ, NX, NC = 4, 16, 4, 2
NT = NX * NC
HEAVY = 12
MOST = 6
PLANE = 35
SENT = 80
KEPT = 128
ROWS, COLS = 8, 256
BF = jnp.bfloat16
F32 = jnp.float32
VMEM = pl.BlockSpec(memory_space=pltpu.VMEM)
SMEM = pl.BlockSpec(memory_space=pltpu.SMEM)
ANY = pl.BlockSpec(memory_space=pl.ANY)
ROOM = pltpu.CompilerParams(vmem_limit_bytes=40 << 20)


def cost(flops, size):
    return pl.CostEstimate(flops=flops, bytes_accessed=size, transcendentals=0)


def dot_t(a, b):
    return lax.dot_general(a, b, (((1,), (1,)), ((), ())), preferred_element_type=F32)


def t_dot(a, b):
    return lax.dot_general(a, b, (((0,), (0,)), ((), ())), preferred_element_type=F32)


def exchange(pieces, axes):
    return lax.all_to_all(pieces, axes, 0, 0, tiled=True)


def spread(piece, axes, n):
    return exchange(jnp.broadcast_to(piece[None], (n,) + piece.shape), axes)


def along_x(array, s):
    return lax.ppermute(array, "x", [(i, (i + s) % NX) for i in range(NX)])


def other_core(array):
    return lax.ppermute(array, "core", [(0, 1), (1, 0)])


def pick_kernel(shard, count, pos, router, tokens, grad_out, out):
    tok_dev, width = tokens.shape
    row = lax.broadcasted_iota(jnp.int32, (8, tok_dev), 0)
    lane = lax.broadcasted_iota(jnp.int32, (8, tok_dev), 1)
    at = jnp.full((8, tok_dev), -1, jnp.int32)
    weight = jnp.zeros((8, tok_dev), F32)
    for j in range(MOST):
        at = jnp.where((row == j) & (j < count[0]), pos[0, j], at)
        weight = jnp.where(row == j, router[0:1, j : j + 1].astype(F32), weight)
    picker = jnp.where(lane == at, 1.0, 0.0).astype(BF)
    meta = jnp.where(lane == 0, weight, 0.0)
    meta = jnp.where(lane == 1, 1.0, meta)
    meta = jnp.where(lane == 2, shard[0].astype(F32), meta)
    meta = jnp.where(lane == 3, row.astype(F32), meta)
    meta = jnp.where(row < count[0], meta, 0.0)
    x = jnp.dot(picker, tokens[...], preferred_element_type=F32)
    dy = jnp.dot(picker, grad_out[...], preferred_element_type=F32)
    both = jnp.concatenate(
        [jnp.concatenate([x, meta], axis=1), jnp.concatenate([dy, meta], axis=1)], axis=0
    ).astype(BF)
    for y in range(NY):
        out[y] = both


def pick_rows(shard, keep_count, keep_pos, router, tokens, grad_out):
    tok_dev, width = tokens.shape
    return pl.pallas_call(
        pick_kernel,
        in_specs=[SMEM, SMEM, SMEM, VMEM, VMEM, VMEM],
        out_specs=VMEM,
        out_shape=jax.ShapeDtypeStruct((NY, 16, width + 128), BF),
        cost_estimate=cost(32 * tok_dev * width, 4 * tok_dev * width),
        name="pick_rows",
    )(shard, keep_count, keep_pos, router, tokens, grad_out)


def select_kernel(where, column, _0, _1, _2, _3, out):
    flat = column[...].reshape(64, column.shape[2])
    m = lax.broadcasted_iota(jnp.int32, (64, 8), 0)
    o = lax.broadcasted_iota(jnp.int32, (64, 8), 1)
    qy, half, qj = m // 16, m // 8 % 2, m % 8
    width = column.shape[2] - 128
    valid = flat[:, width + 1 : width + 2].astype(F32) > 0.5
    heavy = where[1] < HEAVY
    steady = jnp.where(
        heavy,
        jnp.where(qy == 0, jnp.where(qj < MOST, qj, 99), jnp.where(qj == 0, 5 + qy, 99)),
        jnp.where(qj == 0, qy, 99),
    )
    light = jnp.logical_or(qy > 0, jnp.logical_not(heavy))
    extra = jnp.where(valid & (qj >= 1) & light, 1.0, 0.0)
    r = lax.broadcasted_iota(jnp.int32, (64, 64), 0)
    c = lax.broadcasted_iota(jnp.int32, (64, 64), 1)
    before = jnp.where((c < r) & (c // 8 % 2 == r // 8 % 2), 1.0, 0.0).astype(BF)
    nth = jnp.dot(before, extra.astype(BF), preferred_element_type=F32)
    p = o % 4
    turn = lax.rem(where[0] - where[1] + NZ, NY)
    take = jnp.where(
        p < 3,
        jnp.where(steady == 4 * p + turn, 1.0, 0.0),
        jnp.where(nth == where[0].astype(F32), extra, 0.0),
    )
    hot = jnp.where(half == o // 4, take, 0.0).astype(BF)
    picked = t_dot(hot, flat).astype(BF)
    for z in range(NZ):
        out[z] = picked


def select_rows(where, column, after):
    return pl.pallas_call(
        select_kernel,
        in_specs=[SMEM, VMEM] + [ANY] * NX,
        out_specs=VMEM,
        out_shape=jax.ShapeDtypeStruct((NZ, 8, column.shape[2]), BF),
        cost_estimate=cost(16 * column.size, 8 * column.size),
        name="select_rows",
    )(where, column, *after)


def compact_kernel(plane, _1, _2, _3, out):
    width = out.shape[2]
    flat = plane[...].astype(F32).reshape(128, width + 128).astype(BF)
    valid = jnp.where(flat[:, width + 1 : width + 2].astype(F32) > 0.5, 1.0, 0.0)
    r = lax.broadcasted_iota(jnp.int32, (128, 128), 0)
    c = lax.broadcasted_iota(jnp.int32, (128, 128), 1)
    before = jnp.where((c < r) & (c // 4 % 2 == r // 4 % 2), 1.0, 0.0).astype(BF)
    valid = jnp.broadcast_to(valid, (128, 128))
    rank = jnp.dot(before, valid.astype(BF), preferred_element_type=F32)
    rank = rank + jnp.where(r // 4 % 2 == 1, float(PLANE), 0.0)
    hot = jnp.where(rank == c.astype(F32), valid, 0.0).astype(BF)
    rows = t_dot(hot[:, :SENT], flat[:, :width])
    facts = t_dot(flat[:, width:], hot)
    facts = jnp.concatenate([facts[v : v + 1] for v in range(4)], axis=1)
    facts = jnp.concatenate([facts, jnp.zeros((1, width - 512), F32)], axis=1)
    row = lax.broadcasted_iota(jnp.int32, (SENT, width), 0)
    rows = jnp.where(row == 2 * PLANE, facts, rows).astype(BF)
    for y in range(NY):
        out[y] = rows


def compact_rows(plane, after):
    width = plane.shape[2] - 128
    return pl.pallas_call(
        compact_kernel,
        in_specs=[VMEM] + [ANY] * (NX - 1),
        out_specs=VMEM,
        out_shape=jax.ShapeDtypeStruct((NY, SENT, width), BF),
        cost_estimate=cost(256 * plane.size, 8 * plane.size),
        name="compact_rows",
    )(plane, *after)


def run_copies(pairs, sems):
    copies = [
        pltpu.make_async_copy(source, target, sems.at[i])
        for i, (source, target) in enumerate(pairs)
    ]
    for copy in copies:
        copy.start()
    for copy in copies:
        copy.wait()


def peer(place, s, d):
    return lax.rem(place[0] + s + NX, NX) * NC + lax.rem(place[1] + d, NC)


def features(whole, t, width):
    return whole.at[:, pl.ds(pl.multiple_of(t * width, width), width)]


def third(packed, k):
    units = packed.shape[-2] // 3
    return pl.ds(k * units, units)


def pack_kernel(place, gate_w, up_w, down_w, _, out0, out1, out2, out3, sems):
    width = out0.shape[2]
    pairs = []
    for s, out in enumerate((out0, out1, out2, out3)):
        for d in range(NC):
            for k, w in enumerate((gate_w, up_w, down_w)):
                pairs.append((features(w, peer(place, s, d), width), out.at[d, third(out, k)]))
    run_copies(pairs, sems)


def pack_weights(place, gate_weight, up_weight, down_weight, after):
    units, full = gate_weight.shape
    out = jax.ShapeDtypeStruct((NC, 3 * units, full // NT), BF)
    return pl.pallas_call(
        pack_kernel,
        in_specs=[SMEM, ANY, ANY, ANY, ANY],
        out_specs=[VMEM] * NX,
        out_shape=[out] * NX,
        scratch_shapes=[pltpu.SemaphoreType.DMA((3 * NT,))],
        cost_estimate=cost(0, 12 * units * full),
        name="pack_weights",
    )(place, gate_weight, up_weight, down_weight, after)


def join_kernel(in0, in1, in2, in3, out):
    for s, part in enumerate((in0, in1, in2, in3)):
        out[s] = part[0]


def join_far(parts):
    _, units3, width = parts[0].shape
    return pl.pallas_call(
        join_kernel,
        grid=(1,),
        in_specs=[pl.BlockSpec((1, units3, width), lambda i: (1, 0, 0))] * NX,
        out_specs=VMEM,
        out_shape=jax.ShapeDtypeStruct((NX, units3, width), BF),
        cost_estimate=cost(0, 4 * NX * units3 * width),
        name="join_far",
    )(*parts)


def unpack_kernel(place, in0, in1, in2, in3, far, grad_gate, grad_up, grad_down, sems):
    width = far.shape[2]
    pairs = []
    for s, near in enumerate((in0, in1, in2, in3)):
        for d, part in enumerate((near.at[0], far.at[s])):
            for k, out in enumerate((grad_gate, grad_up, grad_down)):
                pairs.append((part.at[third(near, k)], features(out, peer(place, s, d), width)))
    run_copies(pairs, sems)


def unpack_grads(place, parts, far):
    _, units3, width = far.shape
    out = jax.ShapeDtypeStruct((units3 // 3, NT * width), BF)
    return pl.pallas_call(
        unpack_kernel,
        grid=(1,),
        in_specs=[SMEM] + [near_spec(units3, width)] * NX + [VMEM],
        out_specs=[ANY] * 3,
        out_shape=[out] * 3,
        scratch_shapes=[pltpu.SemaphoreType.DMA((3 * NT,))],
        cost_estimate=cost(0, 4 * NT * units3 * width),
        name="unpack_grads",
    )(place, *parts, far)


def near_spec(units3, width):
    return pl.BlockSpec((1, units3, width), lambda i: (0, 0, 0))


def blocks_of(near, far):
    for s in range(NX):
        yield s, 0, near[s][0]
        yield s, 1, far[s]


def forward_kernel(place, slots, messages, w0, w1, w2, w3, far, rows, pre):
    _, units3, width = far.shape
    units = units3 // 3
    slot_id = lax.broadcasted_iota(jnp.int32, (2 * KEPT, SENT), 0)
    total = jnp.zeros((2 * KEPT, width), F32)
    for y in range(NY):
        hot = jnp.where(slot_id == slots[y], 1.0, 0.0).astype(BF)
        total += jnp.dot(hot, messages[y], preferred_element_type=F32)
    ordered = total.astype(BF)
    rows[...] = ordered
    blocks = list(blocks_of((w0, w1, w2, w3), far))
    both = jnp.concatenate([w[: 2 * units] for _, _, w in blocks], axis=0)
    both = dot_t(both, ordered[:KEPT])
    down = jnp.concatenate([w[2 * units :] for _, _, w in blocks], axis=0)
    down = dot_t(down, ordered[KEPT:])
    for i, (s, d, _) in enumerate(blocks):
        t = peer(place, -s, d)
        pre[t, : 2 * units] = both[2 * units * i : 2 * units * (i + 1)]
        pre[t, 2 * units :] = down[units * i : units * (i + 1)]


def forward(place, slots, messages, near, far):
    _, units3, width = far.shape
    return pl.pallas_call(
        forward_kernel,
        grid=(1,),
        in_specs=[SMEM, VMEM, VMEM] + [near_spec(units3, width)] * NX + [VMEM],
        out_specs=[VMEM] * 2,
        out_shape=[
            jax.ShapeDtypeStruct((2 * KEPT, width), BF),
            jax.ShapeDtypeStruct((NT, units3, KEPT), F32),
        ],
        cost_estimate=cost(2 * NT * units3 * width * KEPT, 2 * NT * units3 * width),
        compiler_params=ROOM,
        name="forward",
    )(place, slots, messages, *near, far)


def hidden_kernel(pre, row_scale, out):
    _, units3, _ = pre.shape
    units = units3 // 3
    total = jnp.sum(pre[...], axis=0)
    gate_pre, up_pre, back_proj = total[:units], total[units : 2 * units], total[2 * units :]
    sigmoid_gate = jax.nn.sigmoid(gate_pre)
    activated = gate_pre * sigmoid_gate
    hidden_grad = row_scale[...] * back_proj
    gate = hidden_grad * sigmoid_gate * (1.0 + gate_pre * (1.0 - sigmoid_gate)) * up_pre
    up = hidden_grad * activated
    hidden = activated * up_pre
    both = jnp.concatenate([gate, up, hidden], axis=0).astype(BF)
    for t in range(NT):
        out[t] = both


def hidden_grads(pre, row_scale):
    return pl.pallas_call(
        hidden_kernel,
        in_specs=[VMEM] * 2,
        out_specs=VMEM,
        out_shape=jax.ShapeDtypeStruct(pre.shape, BF),
        cost_estimate=cost(20 * pre.size, 6 * pre.size),
        name="hidden_grads",
    )(pre, row_scale)


def input_grad_kernel(place, grads, w0, w1, w2, w3, far, out):
    _, units3, width = far.shape
    units2 = units3 // 3 * 2
    blocks = list(blocks_of((w0, w1, w2, w3), far))
    g = jnp.concatenate([grads[peer(place, -s, d), :units2] for s, d, _ in blocks], axis=0)
    w = jnp.concatenate([w[:units2] for _, _, w in blocks], axis=0)
    total = t_dot(g, w).astype(BF)
    wide = width // COLS
    for i in range(KEPT // ROWS):
        for k in range(wide):
            out[wide * i + k] = total[ROWS * i : ROWS * (i + 1), COLS * k : COLS * (k + 1)]


def input_grad(place, grads, near, far):
    _, units3, width = far.shape
    pieces = KEPT // ROWS * (width // COLS)
    return pl.pallas_call(
        input_grad_kernel,
        grid=(1,),
        in_specs=[SMEM, VMEM] + [near_spec(units3, width)] * NX + [VMEM],
        out_specs=VMEM,
        out_shape=jax.ShapeDtypeStruct((pieces, ROWS, COLS), BF),
        cost_estimate=cost(2 * NT * units3 * width * KEPT, 2 * NT * units3 * width),
        compiler_params=ROOM,
        name="input_grad",
    )(place, grads, *near, far)


def weight_grads_kernel(place, grads, rows, row_scale, out0, out1, out2, out3):
    _, units3, _ = out0.shape
    units = units3 // 3
    x = rows[:KEPT]
    scaled_dy = (row_scale[...] * rows[KEPT:].astype(F32)).astype(BF)
    for s, out in enumerate((out0, out1, out2, out3)):
        for d in range(NC):
            g = grads[peer(place, -s, d)]
            both = jnp.dot(g[: 2 * units], x, preferred_element_type=F32)
            out[d, : 2 * units] = both.astype(BF)
            down = jnp.dot(g[2 * units :], scaled_dy, preferred_element_type=F32)
            out[d, 2 * units :] = down.astype(BF)


def weight_grads(place, grads, rows, row_scale):
    _, units3, _ = grads.shape
    width = rows.shape[1]
    return pl.pallas_call(
        weight_grads_kernel,
        in_specs=[SMEM] + [VMEM] * 3,
        out_specs=[VMEM] * NX,
        out_shape=[jax.ShapeDtypeStruct((NC, units3, width), BF)] * NX,
        cost_estimate=cost(2 * NT * units3 * width * KEPT, 2 * NT * units3 * width),
        compiler_params=ROOM,
        name="weight_grads",
    )(place, grads, rows, row_scale)


def finish_kernel(blocks, owner, grad_out, grad_tokens, summed):
    width = grad_out.shape[1]
    wide = width // COLS
    rows = []
    for i in range(KEPT // ROWS):
        parts = [blocks[wide * i + k].astype(F32) for k in range(wide)]
        rows.append(jnp.concatenate(parts, axis=1))
    whole = jnp.concatenate(rows, axis=0)
    summed[...] = whole
    added = jnp.dot(owner[...], whole.astype(BF), preferred_element_type=F32)
    grad_tokens[...] = (grad_out[...].astype(F32) + added).astype(BF)


def finish(blocks, owner, grad_out):
    width = grad_out.shape[1]
    return pl.pallas_call(
        finish_kernel,
        in_specs=[VMEM] * 3,
        out_specs=[VMEM] * 2,
        out_shape=[
            jax.ShapeDtypeStruct(grad_out.shape, BF),
            jax.ShapeDtypeStruct((KEPT, width), F32),
        ],
        cost_estimate=cost(2 * KEPT * grad_out.size, 10 * grad_out.size),
        name="finish",
    )(blocks, owner, grad_out)


def body(tokens, grad_out, keep_count, keep_pos, router, gate_weight, up_weight, down_weight):
    tok_dev, width = tokens.shape
    yi, zi = lax.axis_index("y"), lax.axis_index("z")
    place = jnp.stack([lax.axis_index("x"), lax.axis_index("core")])
    shard = yi * NZ + zi
    tensor, context = ("x", "core"), ("y", "z")

    picked = pick_rows(jnp.reshape(shard, (1,)), keep_count, keep_pos, router, tokens, grad_out)
    column = exchange(picked, "y")

    sent = pack_weights(place, gate_weight, up_weight, down_weight, picked)
    near = [sent[0]] + [along_x(sent[s], s) for s in range(1, NX)]
    plane = exchange(select_rows(jnp.stack([yi, zi]), column, sent), "z")
    messages = exchange(compact_rows(plane, near[1:]), "y")
    far = other_core(join_far(near))

    facts = messages[:, 2 * PLANE, :512].reshape(NY, 4, 128).astype(F32)[:, :, :PLANE]
    facts = facts.transpose(1, 0, 2).reshape(4, NY * PLANE)
    valid = facts[1] > 0.5
    key = facts[2] * 8 + facts[3]
    slot = jnp.sum((key[None, :] < key[:, None]) & valid[None, :], axis=1)
    hot = (slot[None, :] == jnp.arange(KEPT)[:, None]) & valid[None, :]
    row_scale = jnp.sum(jnp.where(hot, facts[0][None, :], 0.0), axis=1)
    start_here = jnp.sum((valid & (facts[2] < shard.astype(F32))).astype(jnp.int32))
    slot = jnp.where(valid, slot, -2 * KEPT).reshape(NY, 1, PLANE)
    slot = jnp.pad(
        jnp.concatenate([slot, slot + KEPT], axis=2),
        ((0, 0), (0, 0), (0, SENT - 2 * PLANE)),
        constant_values=-1,
    )

    rows, pre = forward(place, slot, messages, near, far)
    grads = hidden_grads(exchange(pre, tensor), row_scale[None, :])
    grads = exchange(grads, tensor)
    blocks = exchange(input_grad(place, grads, near, far), context)
    units = weight_grads(place, grads, rows, row_scale[:, None])
    units = [units[0]] + [along_x(units[s], -s) for s in range(1, NX)]
    far_units = other_core(join_far(units))
    block = jnp.sum(blocks.astype(F32), axis=0).astype(BF)
    blocks = spread(block, context, NY * NZ)

    j6 = jnp.arange(MOST)
    token_is = (keep_pos[0][None, :] == jnp.arange(tok_dev)[:, None]) & (j6 < keep_count[0])[None, :]
    slot_of = jnp.max(jnp.where(token_is, start_here + j6[None, :], -1), axis=1)
    owner = (slot_of[:, None] == jnp.arange(KEPT)[None, :]).astype(BF)
    grad_tokens, summed = finish(blocks, owner, grad_out)
    grad_gate, grad_up, grad_down = unpack_grads(place, units, far_units)
    return (grad_tokens, grad_gate, grad_up, grad_down, summed)


def solution(mesh):
    grid = Mesh(mesh.devices.reshape(NY, NZ, NX, NC), ("y", "z", "x", "core"))
    context, tensor = ("y", "z"), ("x", "core")
    units = P(tensor + context, None)
    return jax.shard_map(
        body,
        mesh=grid,
        in_specs=(
            P(context, tensor),
            P(context, tensor),
            P(context),
            P(context, None),
            P(context, None),
            units,
            units,
            units,
        ),
        out_specs=(P(context, tensor), units, units, units, P(None, tensor)),
        check_vma=False,
    )
```

```python
import jax
import jax.numpy as jnp
from jax import lax
from jax.experimental import pallas as pl
from jax.experimental.pallas import tpu as pltpu
from jax.sharding import Mesh, PartitionSpec as P

NY, NZ, NX, NC = 4, 16, 4, 2
NT = NX * NC
HEAVY = 12
MOST = 6
PLANE = 35
SENT = 72
KEPT = 128
ROWS, COLS = 8, 256
BF = jnp.bfloat16
F32 = jnp.float32
VMEM = pl.BlockSpec(memory_space=pltpu.VMEM)
SMEM = pl.BlockSpec(memory_space=pltpu.SMEM)
ANY = pl.BlockSpec(memory_space=pl.ANY)
ROOM = pltpu.CompilerParams(vmem_limit_bytes=40 << 20)


def cost(flops, size):
    return pl.CostEstimate(flops=flops, bytes_accessed=size, transcendentals=0)


def dot_t(a, b):
    return lax.dot_general(a, b, (((1,), (1,)), ((), ())), preferred_element_type=F32)


def t_dot(a, b):
    return lax.dot_general(a, b, (((0,), (0,)), ((), ())), preferred_element_type=F32)


def exchange(pieces, axes):
    return lax.all_to_all(pieces, axes, 0, 0, tiled=True)


def spread(piece, axes, n):
    return exchange(jnp.broadcast_to(piece[None], (n,) + piece.shape), axes)


def along_x(array, s):
    return lax.ppermute(array, "x", [(i, (i + s) % NX) for i in range(NX)])


def other_core(array):
    return lax.ppermute(array, "core", [(0, 1), (1, 0)])


def pick_kernel(count, pos, router, tokens, grad_out, out):
    tok_dev, width = tokens.shape
    row = lax.broadcasted_iota(jnp.int32, (8, tok_dev), 0)
    lane = lax.broadcasted_iota(jnp.int32, (8, tok_dev), 1)
    at = jnp.full((8, tok_dev), -1, jnp.int32)
    weight = jnp.zeros((8, tok_dev), F32)
    for j in range(MOST):
        at = jnp.where((row == j) & (j < count[0]), pos[0, j], at)
        weight = jnp.where(row == j, router[0:1, j : j + 1].astype(F32), weight)
    picker = jnp.where(lane == at, 1.0, 0.0).astype(BF)
    meta = jnp.where(lane == 0, weight, 0.0)
    meta = jnp.where(lane == 1, 1.0, meta)
    meta = jnp.where(lane == 3, row.astype(F32), meta)
    meta = jnp.where(row < count[0], meta, 0.0)
    x = jnp.dot(picker, tokens[...], preferred_element_type=F32)
    dy = jnp.dot(picker, grad_out[...], preferred_element_type=F32)
    both = jnp.concatenate(
        [jnp.concatenate([x, meta], axis=1), jnp.concatenate([dy, meta], axis=1)], axis=0
    ).astype(BF)
    for y in range(NY):
        out[y] = both


def pick_rows(keep_count, keep_pos, router, tokens, grad_out):
    tok_dev, width = tokens.shape
    return pl.pallas_call(
        pick_kernel,
        in_specs=[SMEM, SMEM, VMEM, VMEM, VMEM],
        out_specs=VMEM,
        out_shape=jax.ShapeDtypeStruct((NY, 16, width + 128), BF),
        cost_estimate=cost(32 * tok_dev * width, 4 * tok_dev * width),
        name="pick_rows",
    )(keep_count, keep_pos, router, tokens, grad_out)


def select_kernel(place, column, _0, _1, _2, _3, out):
    flat = column[...].reshape(64, column.shape[2])
    width = column.shape[2] - 128
    row = lax.broadcasted_iota(jnp.int32, (64, 128), 0)
    lane = lax.broadcasted_iota(jnp.int32, (64, 128), 1)
    shard = (row // 16 * NZ + place[3]).astype(F32).astype(BF)
    meta = jnp.where(lane == 2, shard, flat[:, width:])
    m = lax.broadcasted_iota(jnp.int32, (64, 8), 0)
    o = lax.broadcasted_iota(jnp.int32, (64, 8), 1)
    qy, half, qj = m // 16, m // 8 % 2, m % 8
    valid = flat[:, width + 1 : width + 2].astype(F32) > 0.5
    heavy = place[3] < HEAVY
    steady = jnp.where(
        heavy,
        jnp.where(qy == 0, jnp.where(qj < MOST, qj, 99), jnp.where(qj == 0, 5 + qy, 99)),
        jnp.where(qj == 0, qy, 99),
    )
    light = jnp.logical_or(qy > 0, jnp.logical_not(heavy))
    extra = jnp.where(valid & (qj >= 1) & light, 1.0, 0.0)
    r = lax.broadcasted_iota(jnp.int32, (64, 64), 0)
    c = lax.broadcasted_iota(jnp.int32, (64, 64), 1)
    before = jnp.where((c < r) & (c // 8 % 2 == r // 8 % 2), 1.0, 0.0).astype(BF)
    nth = jnp.dot(before, extra.astype(BF), preferred_element_type=F32)
    p = o % 4
    turn = lax.rem(place[2] - place[3] + NZ, NY)
    take = jnp.where(
        p < 3,
        jnp.where(steady == 4 * p + turn, 1.0, 0.0),
        jnp.where(nth == place[2].astype(F32), extra, 0.0),
    )
    hot = jnp.where(half == o // 4, take, 0.0).astype(BF)
    picked = t_dot(hot, flat[:, :width]).astype(BF)
    facts = t_dot(hot, meta).astype(BF)
    for z in range(NZ):
        out[z, :, :width] = picked
        out[z, :, width:] = facts


def select_rows(place, column, after):
    return pl.pallas_call(
        select_kernel,
        in_specs=[SMEM, VMEM] + [ANY] * NX,
        out_specs=VMEM,
        out_shape=jax.ShapeDtypeStruct((NZ, 8, column.shape[2]), BF),
        cost_estimate=cost(16 * column.size, 8 * column.size),
        name="select_rows",
    )(place, column, *after)


def compact_kernel(plane, _, out):
    width = out.shape[2]
    flat = plane[...].astype(F32).reshape(128, width + 128).astype(BF)
    valid = jnp.where(flat[:, width + 1 : width + 2].astype(F32) > 0.5, 1.0, 0.0)
    r = lax.broadcasted_iota(jnp.int32, (128, 128), 0)
    c = lax.broadcasted_iota(jnp.int32, (128, 128), 1)
    before = jnp.where((c < r) & (c // 4 % 2 == r // 4 % 2), 1.0, 0.0).astype(BF)
    valid = jnp.broadcast_to(valid, (128, 128))
    rank = jnp.dot(before, valid.astype(BF), preferred_element_type=F32)
    rank = rank + jnp.where(r // 4 % 2 == 1, float(PLANE), 0.0)
    hot = jnp.where(rank == c.astype(F32), valid, 0.0).astype(BF)
    rows = t_dot(hot[:, :SENT], flat[:, :width])
    facts = t_dot(flat[:, width:], hot)
    facts = jnp.concatenate([facts[v : v + 1] for v in range(4)], axis=1)
    facts = jnp.concatenate([facts, jnp.zeros((1, width - 512), F32)], axis=1)
    row = lax.broadcasted_iota(jnp.int32, (SENT, width), 0)
    rows = jnp.where(row == 2 * PLANE, facts, rows).astype(BF)
    for y in range(NY):
        out[y] = rows


def compact_rows(plane, after):
    width = plane.shape[2] - 128
    return pl.pallas_call(
        compact_kernel,
        in_specs=[VMEM, ANY],
        out_specs=VMEM,
        out_shape=jax.ShapeDtypeStruct((NY, SENT, width), BF),
        cost_estimate=cost(256 * plane.size, 8 * plane.size),
        name="compact_rows",
    )(plane, after)


def run_copies(pairs, sems):
    copies = [
        pltpu.make_async_copy(source, target, sems.at[i])
        for i, (source, target) in enumerate(pairs)
    ]
    for copy in copies:
        copy.start()
    for copy in copies:
        copy.wait()


def peer(place, s, d):
    return lax.rem(place[0] + s + NX, NX) * NC + lax.rem(place[1] + d, NC)


def features(whole, t, width):
    return whole.at[:, pl.ds(pl.multiple_of(t * width, width), width)]


def third(packed, k):
    units = packed.shape[-2] // 3
    return pl.ds(k * units, units)


def pack_kernel(place, gate_w, up_w, down_w, _, out0, out1, out2, out3, sems):
    width = out0.shape[2]
    pairs = []
    for s, out in enumerate((out0, out1, out2, out3)):
        for d in range(NC):
            for k, w in enumerate((gate_w, up_w, down_w)):
                pairs.append((features(w, peer(place, s, d), width), out.at[d, third(out, k)]))
    run_copies(pairs, sems)


def pack_weights(place, gate_weight, up_weight, down_weight, after):
    units, full = gate_weight.shape
    out = jax.ShapeDtypeStruct((NC, 3 * units, full // NT), BF)
    return pl.pallas_call(
        pack_kernel,
        in_specs=[SMEM, ANY, ANY, ANY, ANY],
        out_specs=[VMEM] * NX,
        out_shape=[out] * NX,
        scratch_shapes=[pltpu.SemaphoreType.DMA((3 * NT,))],
        cost_estimate=cost(0, 12 * units * full),
        name="pack_weights",
    )(place, gate_weight, up_weight, down_weight, after)


def join_kernel(*refs):
    out = refs[-1]
    for s, part in enumerate(refs[:-1]):
        out[s] = part[0]


def join_far(parts):
    n = len(parts)
    _, units3, width = parts[0].shape
    return pl.pallas_call(
        join_kernel,
        grid=(1,),
        in_specs=[pl.BlockSpec((1, units3, width), lambda i: (1, 0, 0))] * n,
        out_specs=VMEM,
        out_shape=jax.ShapeDtypeStruct((n, units3, width), BF),
        cost_estimate=cost(0, 4 * n * units3 * width),
        name="join_far",
    )(*parts)


def unpack_kernel(place, in0, in1, in2, in3, far, grad_gate, grad_up, grad_down, sems):
    width = far.shape[2]
    pairs = []
    for s, near in enumerate((in0, in1, in2, in3)):
        for d, part in enumerate((near.at[0], far.at[s])):
            for k, out in enumerate((grad_gate, grad_up, grad_down)):
                pairs.append((part.at[third(near, k)], features(out, peer(place, s, d), width)))
    run_copies(pairs, sems)


def unpack_grads(place, parts, far):
    _, units3, width = far.shape
    out = jax.ShapeDtypeStruct((units3 // 3, NT * width), BF)
    return pl.pallas_call(
        unpack_kernel,
        grid=(1,),
        in_specs=[SMEM] + [near_spec(units3, width)] * NX + [VMEM],
        out_specs=[ANY] * 3,
        out_shape=[out] * 3,
        scratch_shapes=[pltpu.SemaphoreType.DMA((3 * NT,))],
        cost_estimate=cost(0, 4 * NT * units3 * width),
        name="unpack_grads",
    )(place, *parts, far)


def near_spec(units3, width):
    return pl.BlockSpec((1, units3, width), lambda i: (0, 0, 0))


def blocks_of(near, far):
    for s in range(NX):
        yield s, 0, near[s][0]
        yield s, 1, far[s]


def slots_of(messages):
    lane = lax.broadcasted_iota(jnp.int32, (1, 128), 1)
    rows = []
    for y in range(NY):
        facts = messages[y][2 * PLANE : 2 * PLANE + 1, :512].astype(F32)
        key = facts[:, 256:384] * 8.0 + facts[:, 384:512]
        rows.append(jnp.where(facts[:, 128:256] > 0.5, key, 1e6))
    keys = jnp.concatenate([jnp.where(lane < PLANE, r, 1e6) for r in rows] * 2, axis=0).T
    for key in rows:
        slot = jnp.zeros((1, 128), F32)
        for y in range(NY):
            less = jnp.where(keys[:, y : y + 1] < key, 1.0, 0.0)
            slot += jnp.sum(less, axis=0, keepdims=True)
        yield jnp.where(key < 1e5, slot, -1000.0).astype(jnp.int32)


def order_rows(messages):
    lane = lax.broadcasted_iota(jnp.int32, (2 * KEPT, 128), 1)
    slot_id = lax.broadcasted_iota(jnp.int32, (2 * KEPT, 128), 0)
    slot_id = slot_id - jnp.where(lane < PLANE, 0, KEPT)
    total = jnp.zeros((2 * KEPT, messages.shape[2]), F32)
    for y, slots in enumerate(slots_of(messages)):
        hot = jnp.where(slot_id == slots, 1.0, 0.0).astype(BF)[:, :SENT]
        total += jnp.dot(hot, messages[y], preferred_element_type=F32)
    return total.astype(BF)


def forward_kernel(place, messages, w0, w1, w2, w3, far, pre):
    _, units3, width = far.shape
    units = units3 // 3
    ordered = order_rows(messages)
    blocks = list(blocks_of((w0, w1, w2, w3), far))
    both = jnp.concatenate([w[: 2 * units] for _, _, w in blocks], axis=0)
    both = dot_t(both, ordered[:KEPT])
    down = jnp.concatenate([w[2 * units :] for _, _, w in blocks], axis=0)
    down = dot_t(down, ordered[KEPT:])
    for i, (s, d, _) in enumerate(blocks):
        t = peer(place, -s, d)
        pre[t, : 2 * units] = both[2 * units * i : 2 * units * (i + 1)]
        pre[t, 2 * units :] = down[units * i : units * (i + 1)]


def forward(place, messages, near, far):
    _, units3, width = far.shape
    return pl.pallas_call(
        forward_kernel,
        grid=(1,),
        in_specs=[SMEM, VMEM] + [near_spec(units3, width)] * NX + [VMEM],
        out_specs=VMEM,
        out_shape=jax.ShapeDtypeStruct((NT, units3, KEPT), F32),
        cost_estimate=cost(2 * NT * units3 * width * KEPT, 2 * NT * units3 * width),
        compiler_params=ROOM,
        name="forward",
    )(place, messages, *near, far)


def hidden_kernel(pre, row_scale, out):
    _, units3, _ = pre.shape
    units = units3 // 3
    total = jnp.sum(pre[...], axis=0)
    gate_pre, up_pre, back_proj = total[:units], total[units : 2 * units], total[2 * units :]
    sigmoid_gate = jax.nn.sigmoid(gate_pre)
    activated = gate_pre * sigmoid_gate
    hidden_grad = row_scale[...] * back_proj
    gate = hidden_grad * sigmoid_gate * (1.0 + gate_pre * (1.0 - sigmoid_gate)) * up_pre
    up = hidden_grad * activated
    hidden = activated * up_pre
    both = jnp.concatenate([gate, up, hidden], axis=0).astype(BF)
    for t in range(NT):
        out[t] = both


def hidden_grads(pre, row_scale):
    return pl.pallas_call(
        hidden_kernel,
        in_specs=[VMEM] * 2,
        out_specs=VMEM,
        out_shape=jax.ShapeDtypeStruct(pre.shape, BF),
        cost_estimate=cost(20 * pre.size, 6 * pre.size),
        name="hidden_grads",
    )(pre, row_scale)


def input_grad_kernel(place, grads, w0, w1, w2, w3, far, out):
    _, units3, width = far.shape
    units2 = units3 // 3 * 2
    blocks = list(blocks_of((w0, w1, w2, w3), far))
    g = jnp.concatenate([grads[peer(place, -s, d), :units2] for s, d, _ in blocks], axis=0)
    w = jnp.concatenate([w[:units2] for _, _, w in blocks], axis=0)
    total = t_dot(g, w).astype(BF)
    wide = width // COLS
    for i in range(KEPT // ROWS):
        for k in range(wide):
            out[wide * i + k] = total[ROWS * i : ROWS * (i + 1), COLS * k : COLS * (k + 1)]


def input_grad(place, grads, near, far):
    _, units3, width = far.shape
    pieces = KEPT // ROWS * (width // COLS)
    return pl.pallas_call(
        input_grad_kernel,
        grid=(1,),
        in_specs=[SMEM, VMEM] + [near_spec(units3, width)] * NX + [VMEM],
        out_specs=VMEM,
        out_shape=jax.ShapeDtypeStruct((pieces, ROWS, COLS), BF),
        cost_estimate=cost(2 * NT * units3 * width * KEPT, 2 * NT * units3 * width),
        compiler_params=ROOM,
        name="input_grad",
    )(place, grads, *near, far)


def weight_grads_kernel(place, grads, messages, row_scale, out0, out1, out2, out3):
    _, units3, _ = out0.shape
    units = units3 // 3
    rows = order_rows(messages)
    x = rows[:KEPT]
    scaled_dy = (row_scale[...] * rows[KEPT:].astype(F32)).astype(BF)
    for s, out in enumerate((out0, out1, out2, out3)):
        for d in range(NC):
            g = grads[peer(place, -s, d)]
            both = jnp.dot(g[: 2 * units], x, preferred_element_type=F32)
            out[d, : 2 * units] = both.astype(BF)
            down = jnp.dot(g[2 * units :], scaled_dy, preferred_element_type=F32)
            out[d, 2 * units :] = down.astype(BF)


def weight_grads(place, grads, messages, row_scale):
    _, units3, _ = grads.shape
    width = messages.shape[2]
    return pl.pallas_call(
        weight_grads_kernel,
        in_specs=[SMEM] + [VMEM] * 3,
        out_specs=[VMEM] * NX,
        out_shape=[jax.ShapeDtypeStruct((NC, units3, width), BF)] * NX,
        cost_estimate=cost(2 * NT * units3 * width * KEPT, 2 * NT * units3 * width),
        compiler_params=ROOM,
        name="weight_grads",
    )(place, grads, messages, row_scale)


def finish_kernel(blocks, owner, grad_out, grad_tokens, summed):
    width = grad_out.shape[1]
    wide = width // COLS
    rows = []
    for i in range(KEPT // ROWS):
        parts = [blocks[wide * i + k].astype(F32) for k in range(wide)]
        rows.append(jnp.concatenate(parts, axis=1))
    whole = jnp.concatenate(rows, axis=0)
    summed[...] = whole
    added = jnp.dot(owner[...], whole.astype(BF), preferred_element_type=F32)
    grad_tokens[...] = (grad_out[...].astype(F32) + added).astype(BF)


def finish(blocks, owner, grad_out):
    width = grad_out.shape[1]
    return pl.pallas_call(
        finish_kernel,
        in_specs=[VMEM] * 3,
        out_specs=[VMEM] * 2,
        out_shape=[
            jax.ShapeDtypeStruct(grad_out.shape, BF),
            jax.ShapeDtypeStruct((KEPT, width), F32),
        ],
        cost_estimate=cost(2 * KEPT * grad_out.size, 10 * grad_out.size),
        name="finish",
    )(blocks, owner, grad_out)


def body(tokens, grad_out, keep_count, keep_pos, router, gate_weight, up_weight, down_weight):
    tok_dev, width = tokens.shape
    yi, zi = lax.axis_index("y"), lax.axis_index("z")
    shard = yi * NZ + zi
    place = jnp.stack([lax.axis_index("x"), lax.axis_index("core"), yi, zi])
    tensor, context = ("x", "core"), ("y", "z")

    picked = pick_rows(keep_count, keep_pos, router, tokens, grad_out)
    column = exchange(picked, "y")

    sent = pack_weights(place, gate_weight, up_weight, down_weight, picked)
    near = [sent[0]] + [along_x(sent[s], s) for s in range(1, NX)]
    far = other_core(join_far(near))
    plane = exchange(select_rows(place, column, sent), "z")
    messages = exchange(compact_rows(plane, far), "y")

    facts = messages[:, 2 * PLANE, :512].reshape(NY, 4, 128).astype(F32)[:, :, :PLANE]
    facts = facts.transpose(1, 0, 2).reshape(4, NY * PLANE)
    valid = facts[1] > 0.5
    key = facts[2] * 8 + facts[3]
    slot = jnp.sum((key[None, :] < key[:, None]) & valid[None, :], axis=1)
    hot = (slot[None, :] == jnp.arange(KEPT)[:, None]) & valid[None, :]
    row_scale = jnp.sum(jnp.where(hot, facts[0][None, :], 0.0), axis=1)
    start_here = jnp.sum((valid & (facts[2] < shard.astype(F32))).astype(jnp.int32))

    pre = forward(place, messages, near, far)
    grads = hidden_grads(exchange(pre, tensor), row_scale[None, :])
    grads = exchange(grads, tensor)
    blocks = exchange(input_grad(place, grads, near, far), context)
    units = weight_grads(place, grads, messages, row_scale[:, None])
    units = [units[0]] + [along_x(units[s], -s) for s in range(1, NX)]
    far_units = other_core(join_far(units))
    block = jnp.sum(blocks.astype(F32), axis=0).astype(BF)
    blocks = spread(block, context, NY * NZ)

    j6 = jnp.arange(MOST)
    token_is = (keep_pos[0][None, :] == jnp.arange(tok_dev)[:, None]) & (j6 < keep_count[0])[None, :]
    slot_of = jnp.max(jnp.where(token_is, start_here + j6[None, :], -1), axis=1)
    owner = (slot_of[:, None] == jnp.arange(KEPT)[None, :]).astype(BF)
    grad_tokens, summed = finish(blocks, owner, grad_out)
    grad_gate, grad_up, grad_down = unpack_grads(place, units, far_units)
    return (grad_tokens, grad_gate, grad_up, grad_down, summed)


def solution(mesh):
    grid = Mesh(mesh.devices.reshape(NY, NZ, NX, NC), ("y", "z", "x", "core"))
    context, tensor = ("y", "z"), ("x", "core")
    units = P(tensor + context, None)
    return jax.shard_map(
        body,
        mesh=grid,
        in_specs=(
            P(context, tensor),
            P(context, tensor),
            P(context),
            P(context, None),
            P(context, None),
            units,
            units,
            units,
        ),
        out_specs=(P(context, tensor), units, units, units, P(None, tensor)),
        check_vma=False,
    )
```

```python
import jax
import jax.numpy as jnp
from jax import lax
from jax.experimental import pallas as pl
from jax.experimental.pallas import tpu as pltpu
from jax.sharding import Mesh, PartitionSpec as P

NY, NZ, NX, NC = 4, 16, 4, 2
NT = NX * NC
HEAVY = 12
MOST = 6
PLANE = 35
SENT = 72
KEPT = 128
ROWS, COLS = 8, 256
BF = jnp.bfloat16
F32 = jnp.float32
VMEM = pl.BlockSpec(memory_space=pltpu.VMEM)
SMEM = pl.BlockSpec(memory_space=pltpu.SMEM)
ANY = pl.BlockSpec(memory_space=pl.ANY)
ROOM = pltpu.CompilerParams(vmem_limit_bytes=40 << 20)


def cost(flops, size):
    return pl.CostEstimate(flops=flops, bytes_accessed=size, transcendentals=0)


def dot_t(a, b):
    return lax.dot_general(a, b, (((1,), (1,)), ((), ())), preferred_element_type=F32)


def t_dot(a, b):
    return lax.dot_general(a, b, (((0,), (0,)), ((), ())), preferred_element_type=F32)


def exchange(pieces, axes):
    return lax.all_to_all(pieces, axes, 0, 0, tiled=True)


def spread(piece, axes, n):
    return exchange(jnp.broadcast_to(piece[None], (n,) + piece.shape), axes)


def along_x(array, s):
    return lax.ppermute(array, "x", [(i, (i + s) % NX) for i in range(NX)])


def other_core(array):
    return lax.ppermute(array, "core", [(0, 1), (1, 0)])


def pick_kernel(count, pos, router, tokens, grad_out, out):
    tok_dev, width = tokens.shape
    row = lax.broadcasted_iota(jnp.int32, (8, tok_dev), 0)
    lane = lax.broadcasted_iota(jnp.int32, (8, tok_dev), 1)
    at = jnp.full((8, tok_dev), -1, jnp.int32)
    weight = jnp.zeros((8, tok_dev), F32)
    for j in range(MOST):
        at = jnp.where((row == j) & (j < count[0]), pos[0, j], at)
        weight = jnp.where(row == j, router[0:1, j : j + 1].astype(F32), weight)
    picker = jnp.where(lane == at, 1.0, 0.0).astype(BF)
    meta = jnp.where(lane == 0, weight, 0.0)
    meta = jnp.where(lane == 1, 1.0, meta)
    meta = jnp.where(lane == 3, row.astype(F32), meta)
    meta = jnp.where(row < count[0], meta, 0.0)
    x = jnp.dot(picker, tokens[...], preferred_element_type=F32)
    dy = jnp.dot(picker, grad_out[...], preferred_element_type=F32)
    both = jnp.concatenate(
        [jnp.concatenate([x, meta], axis=1), jnp.concatenate([dy, meta], axis=1)], axis=0
    ).astype(BF)
    for y in range(NY):
        out[y] = both


def pick_rows(keep_count, keep_pos, router, tokens, grad_out):
    tok_dev, width = tokens.shape
    return pl.pallas_call(
        pick_kernel,
        in_specs=[SMEM, SMEM, VMEM, VMEM, VMEM],
        out_specs=VMEM,
        out_shape=jax.ShapeDtypeStruct((NY, 16, width + 128), BF),
        cost_estimate=cost(32 * tok_dev * width, 4 * tok_dev * width),
        name="pick_rows",
    )(keep_count, keep_pos, router, tokens, grad_out)


def select_kernel(column, out):
    yi, zi = lax.axis_index("y"), lax.axis_index("z")
    flat = column[...].reshape(64, column.shape[2])
    width = column.shape[2] - 128
    row = lax.broadcasted_iota(jnp.int32, (64, 128), 0)
    lane = lax.broadcasted_iota(jnp.int32, (64, 128), 1)
    shard = (row // 16 * NZ + zi).astype(F32).astype(BF)
    meta = jnp.where(lane == 2, shard, flat[:, width:])
    m = lax.broadcasted_iota(jnp.int32, (64, 8), 0)
    o = lax.broadcasted_iota(jnp.int32, (64, 8), 1)
    qy, half, qj = m // 16, m // 8 % 2, m % 8
    valid = flat[:, width + 1 : width + 2].astype(F32) > 0.5
    heavy = zi < HEAVY
    steady = jnp.where(
        heavy,
        jnp.where(qy == 0, jnp.where(qj < MOST, qj, 99), jnp.where(qj == 0, 5 + qy, 99)),
        jnp.where(qj == 0, qy, 99),
    )
    light = jnp.logical_or(qy > 0, jnp.logical_not(heavy))
    extra = jnp.where(valid & (qj >= 1) & light, 1.0, 0.0)
    r = lax.broadcasted_iota(jnp.int32, (64, 64), 0)
    c = lax.broadcasted_iota(jnp.int32, (64, 64), 1)
    before = jnp.where((c < r) & (c // 8 % 2 == r // 8 % 2), 1.0, 0.0).astype(BF)
    nth = jnp.dot(before, extra.astype(BF), preferred_element_type=F32)
    p = o % 4
    turn = lax.rem(yi - zi + NZ, NY)
    take = jnp.where(
        p < 3,
        jnp.where(steady == 4 * p + turn, 1.0, 0.0),
        jnp.where(nth == yi.astype(F32), extra, 0.0),
    )
    hot = jnp.where(half == o // 4, take, 0.0).astype(BF)
    picked = t_dot(hot, flat[:, :width]).astype(BF)
    facts = t_dot(hot, meta).astype(BF)
    for z in range(NZ):
        out[z, :, :width] = picked
        out[z, :, width:] = facts


def select_rows(column):
    return pl.pallas_call(
        select_kernel,
        in_specs=[VMEM],
        out_specs=VMEM,
        out_shape=jax.ShapeDtypeStruct((NZ, 8, column.shape[2]), BF),
        cost_estimate=cost(16 * column.size, 8 * column.size),
        name="select_rows",
    )(column)


def compact_kernel(plane, _, out):
    width = out.shape[2]
    flat = plane[...].astype(F32).reshape(128, width + 128).astype(BF)
    valid = jnp.where(flat[:, width + 1 : width + 2].astype(F32) > 0.5, 1.0, 0.0)
    r = lax.broadcasted_iota(jnp.int32, (128, 128), 0)
    c = lax.broadcasted_iota(jnp.int32, (128, 128), 1)
    before = jnp.where((c < r) & (c // 4 % 2 == r // 4 % 2), 1.0, 0.0).astype(BF)
    valid = jnp.broadcast_to(valid, (128, 128))
    rank = jnp.dot(before, valid.astype(BF), preferred_element_type=F32)
    rank = rank + jnp.where(r // 4 % 2 == 1, float(PLANE), 0.0)
    hot = jnp.where(rank == c.astype(F32), valid, 0.0).astype(BF)
    rows = t_dot(hot[:, :SENT], flat[:, :width])
    facts = t_dot(flat[:, width:], hot)
    facts = jnp.concatenate([facts[v : v + 1] for v in range(4)], axis=1)
    facts = jnp.concatenate([facts, jnp.zeros((1, width - 512), F32)], axis=1)
    row = lax.broadcasted_iota(jnp.int32, (SENT, width), 0)
    rows = jnp.where(row == 2 * PLANE, facts, rows).astype(BF)
    for y in range(NY):
        out[y] = rows


def compact_rows(plane, after):
    width = plane.shape[2] - 128
    return pl.pallas_call(
        compact_kernel,
        in_specs=[VMEM, ANY],
        out_specs=VMEM,
        out_shape=jax.ShapeDtypeStruct((NY, SENT, width), BF),
        cost_estimate=cost(256 * plane.size, 8 * plane.size),
        name="compact_rows",
    )(plane, after)


def run_copies(pairs, sems):
    copies = [
        pltpu.make_async_copy(source, target, sems.at[i])
        for i, (source, target) in enumerate(pairs)
    ]
    for copy in copies:
        copy.start()
    for copy in copies:
        copy.wait()


def peer(s, d):
    x, core = lax.axis_index("x"), lax.axis_index("core")
    return lax.rem(x + s + NX, NX) * NC + lax.rem(core + d, NC)


def features(whole, t, width):
    return whole.at[:, pl.ds(pl.multiple_of(t * width, width), width)]


def third(packed, k):
    units = packed.shape[-2] // 3
    return pl.ds(k * units, units)


def pack_kernel(gate_w, up_w, down_w, _, out0, out1, out2, out3, sems):
    width = out0.shape[2]
    pairs = []
    for s, out in enumerate((out0, out1, out2, out3)):
        for d in range(NC):
            for k, w in enumerate((gate_w, up_w, down_w)):
                pairs.append((features(w, peer(s, d), width), out.at[d, third(out, k)]))
    run_copies(pairs, sems)


def pack_weights(gate_weight, up_weight, down_weight, after):
    units, full = gate_weight.shape
    out = jax.ShapeDtypeStruct((NC, 3 * units, full // NT), BF)
    return pl.pallas_call(
        pack_kernel,
        in_specs=[ANY] * 4,
        out_specs=[VMEM] * NX,
        out_shape=[out] * NX,
        scratch_shapes=[pltpu.SemaphoreType.DMA((3 * NT,))],
        cost_estimate=cost(0, 12 * units * full),
        name="pack_weights",
    )(gate_weight, up_weight, down_weight, after)


def join_kernel(*refs):
    out = refs[-1]
    for s, part in enumerate(refs[:-1]):
        out[s] = part[0]


def join_far(parts):
    n = len(parts)
    _, units3, width = parts[0].shape
    return pl.pallas_call(
        join_kernel,
        grid=(1,),
        in_specs=[pl.BlockSpec((1, units3, width), lambda i: (1, 0, 0))] * n,
        out_specs=VMEM,
        out_shape=jax.ShapeDtypeStruct((n, units3, width), BF),
        cost_estimate=cost(0, 4 * n * units3 * width),
        name="join_far",
    )(*parts)


def unpack_kernel(in0, in1, in2, in3, far, grad_gate, grad_up, grad_down, sems):
    width = far.shape[2]
    pairs = []
    for s, near in enumerate((in0, in1, in2, in3)):
        for d, part in enumerate((near.at[0], far.at[s])):
            for k, out in enumerate((grad_gate, grad_up, grad_down)):
                pairs.append((part.at[third(near, k)], features(out, peer(s, d), width)))
    run_copies(pairs, sems)


def unpack_grads(parts, far):
    _, units3, width = far.shape
    out = jax.ShapeDtypeStruct((units3 // 3, NT * width), BF)
    return pl.pallas_call(
        unpack_kernel,
        grid=(1,),
        in_specs=[near_spec(units3, width)] * NX + [VMEM],
        out_specs=[ANY] * 3,
        out_shape=[out] * 3,
        scratch_shapes=[pltpu.SemaphoreType.DMA((3 * NT,))],
        cost_estimate=cost(0, 4 * NT * units3 * width),
        name="unpack_grads",
    )(*parts, far)


def near_spec(units3, width):
    return pl.BlockSpec((1, units3, width), lambda i: (0, 0, 0))


def blocks_of(near, far):
    for s in range(NX):
        yield s, 0, near[s][0]
        yield s, 1, far[s]


def slots_of(messages):
    lane = lax.broadcasted_iota(jnp.int32, (1, 128), 1)
    rows = []
    for y in range(NY):
        facts = messages[y][2 * PLANE : 2 * PLANE + 1, :512].astype(F32)
        key = facts[:, 256:384] * 8.0 + facts[:, 384:512]
        rows.append(jnp.where(facts[:, 128:256] > 0.5, key, 1e6))
    keys = jnp.concatenate([jnp.where(lane < PLANE, r, 1e6) for r in rows] * 2, axis=0).T
    for key in rows:
        slot = jnp.zeros((1, 128), F32)
        for y in range(NY):
            less = jnp.where(keys[:, y : y + 1] < key, 1.0, 0.0)
            slot += jnp.sum(less, axis=0, keepdims=True)
        yield jnp.where(key < 1e5, slot, -1000.0).astype(jnp.int32)


def order_rows(messages):
    lane = lax.broadcasted_iota(jnp.int32, (2 * KEPT, 128), 1)
    slot_id = lax.broadcasted_iota(jnp.int32, (2 * KEPT, 128), 0)
    slot_id = slot_id - jnp.where(lane < PLANE, 0, KEPT)
    total = jnp.zeros((2 * KEPT, messages.shape[2]), F32)
    for y, slots in enumerate(slots_of(messages)):
        hot = jnp.where(slot_id == slots, 1.0, 0.0).astype(BF)[:, :SENT]
        total += jnp.dot(hot, messages[y], preferred_element_type=F32)
    return total.astype(BF)


def forward_kernel(messages, w0, w1, w2, w3, far, pre):
    _, units3, width = far.shape
    units = units3 // 3
    ordered = order_rows(messages)
    blocks = list(blocks_of((w0, w1, w2, w3), far))
    both = jnp.concatenate([w[: 2 * units] for _, _, w in blocks], axis=0)
    both = dot_t(both, ordered[:KEPT])
    down = jnp.concatenate([w[2 * units :] for _, _, w in blocks], axis=0)
    down = dot_t(down, ordered[KEPT:])
    for i, (s, d, _) in enumerate(blocks):
        t = peer(-s, d)
        pre[t, : 2 * units] = both[2 * units * i : 2 * units * (i + 1)]
        pre[t, 2 * units :] = down[units * i : units * (i + 1)]


def forward(messages, near, far):
    _, units3, width = far.shape
    return pl.pallas_call(
        forward_kernel,
        grid=(1,),
        in_specs=[VMEM] + [near_spec(units3, width)] * NX + [VMEM],
        out_specs=VMEM,
        out_shape=jax.ShapeDtypeStruct((NT, units3, KEPT), F32),
        cost_estimate=cost(2 * NT * units3 * width * KEPT, 2 * NT * units3 * width),
        compiler_params=ROOM,
        name="forward",
    )(messages, *near, far)


def hidden_kernel(pre, row_scale, out):
    _, units3, _ = pre.shape
    units = units3 // 3
    total = jnp.sum(pre[...], axis=0)
    gate_pre, up_pre, back_proj = total[:units], total[units : 2 * units], total[2 * units :]
    sigmoid_gate = jax.nn.sigmoid(gate_pre)
    activated = gate_pre * sigmoid_gate
    hidden_grad = row_scale[...] * back_proj
    gate = hidden_grad * sigmoid_gate * (1.0 + gate_pre * (1.0 - sigmoid_gate)) * up_pre
    up = hidden_grad * activated
    hidden = activated * up_pre
    both = jnp.concatenate([gate, up, hidden], axis=0).astype(BF)
    for t in range(NT):
        out[t] = both


def hidden_grads(pre, row_scale):
    return pl.pallas_call(
        hidden_kernel,
        in_specs=[VMEM] * 2,
        out_specs=VMEM,
        out_shape=jax.ShapeDtypeStruct(pre.shape, BF),
        cost_estimate=cost(20 * pre.size, 6 * pre.size),
        name="hidden_grads",
    )(pre, row_scale)


def input_grad_kernel(grads, w0, w1, w2, w3, far, out):
    _, units3, width = far.shape
    units2 = units3 // 3 * 2
    blocks = list(blocks_of((w0, w1, w2, w3), far))
    g = jnp.concatenate([grads[peer(-s, d), :units2] for s, d, _ in blocks], axis=0)
    w = jnp.concatenate([w[:units2] for _, _, w in blocks], axis=0)
    total = t_dot(g, w).astype(BF)
    wide = width // COLS
    for i in range(KEPT // ROWS):
        for k in range(wide):
            out[wide * i + k] = total[ROWS * i : ROWS * (i + 1), COLS * k : COLS * (k + 1)]


def input_grad(grads, near, far):
    _, units3, width = far.shape
    pieces = KEPT // ROWS * (width // COLS)
    return pl.pallas_call(
        input_grad_kernel,
        grid=(1,),
        in_specs=[VMEM] + [near_spec(units3, width)] * NX + [VMEM],
        out_specs=VMEM,
        out_shape=jax.ShapeDtypeStruct((pieces, ROWS, COLS), BF),
        cost_estimate=cost(2 * NT * units3 * width * KEPT, 2 * NT * units3 * width),
        compiler_params=ROOM,
        name="input_grad",
    )(grads, *near, far)


def weight_grads_kernel(grads, messages, row_scale, out0, out1, out2, out3):
    _, units3, _ = out0.shape
    units = units3 // 3
    rows = order_rows(messages)
    x = rows[:KEPT]
    scaled_dy = (row_scale[...] * rows[KEPT:].astype(F32)).astype(BF)
    for s, out in enumerate((out0, out1, out2, out3)):
        for d in range(NC):
            g = grads[peer(-s, d)]
            both = jnp.dot(g[: 2 * units], x, preferred_element_type=F32)
            out[d, : 2 * units] = both.astype(BF)
            down = jnp.dot(g[2 * units :], scaled_dy, preferred_element_type=F32)
            out[d, 2 * units :] = down.astype(BF)


def weight_grads(grads, messages, row_scale):
    _, units3, _ = grads.shape
    width = messages.shape[2]
    return pl.pallas_call(
        weight_grads_kernel,
        in_specs=[VMEM] * 3,
        out_specs=[VMEM] * NX,
        out_shape=[jax.ShapeDtypeStruct((NC, units3, width), BF)] * NX,
        cost_estimate=cost(2 * NT * units3 * width * KEPT, 2 * NT * units3 * width),
        compiler_params=ROOM,
        name="weight_grads",
    )(grads, messages, row_scale)


def finish_kernel(blocks, owner, grad_out, grad_tokens, summed):
    width = grad_out.shape[1]
    wide = width // COLS
    rows = []
    for i in range(KEPT // ROWS):
        parts = [blocks[wide * i + k].astype(F32) for k in range(wide)]
        rows.append(jnp.concatenate(parts, axis=1))
    whole = jnp.concatenate(rows, axis=0)
    summed[...] = whole
    added = jnp.dot(owner[...], whole.astype(BF), preferred_element_type=F32)
    grad_tokens[...] = (grad_out[...].astype(F32) + added).astype(BF)


def finish(blocks, owner, grad_out):
    width = grad_out.shape[1]
    return pl.pallas_call(
        finish_kernel,
        in_specs=[VMEM] * 3,
        out_specs=[VMEM] * 2,
        out_shape=[
            jax.ShapeDtypeStruct(grad_out.shape, BF),
            jax.ShapeDtypeStruct((KEPT, width), F32),
        ],
        cost_estimate=cost(2 * KEPT * grad_out.size, 10 * grad_out.size),
        name="finish",
    )(blocks, owner, grad_out)


def body(tokens, grad_out, keep_count, keep_pos, router, gate_weight, up_weight, down_weight):
    tok_dev, width = tokens.shape
    yi, zi = lax.axis_index("y"), lax.axis_index("z")
    shard = yi * NZ + zi
    tensor, context = ("x", "core"), ("y", "z")

    picked = pick_rows(keep_count, keep_pos, router, tokens, grad_out)
    column = exchange(picked, "y")

    sent = pack_weights(gate_weight, up_weight, down_weight, picked)
    near = [sent[0]] + [along_x(sent[s], s) for s in range(1, NX)]
    far = other_core(join_far(near))
    plane = exchange(select_rows(column), "z")
    messages = exchange(compact_rows(plane, far), "y")

    facts = messages[:, 2 * PLANE, :512].reshape(NY, 4, 128).astype(F32)[:, :, :PLANE]
    facts = facts.transpose(1, 0, 2).reshape(4, NY * PLANE)
    valid = facts[1] > 0.5
    key = facts[2] * 8 + facts[3]
    slot = jnp.sum((key[None, :] < key[:, None]) & valid[None, :], axis=1)
    hot = (slot[None, :] == jnp.arange(KEPT)[:, None]) & valid[None, :]
    row_scale = jnp.sum(jnp.where(hot, facts[0][None, :], 0.0), axis=1)
    start_here = jnp.sum((valid & (facts[2] < shard.astype(F32))).astype(jnp.int32))

    pre = forward(messages, near, far)
    grads = hidden_grads(exchange(pre, tensor), row_scale[None, :])
    grads = exchange(grads, tensor)
    blocks = exchange(input_grad(grads, near, far), context)
    units = weight_grads(grads, messages, row_scale[:, None])
    units = [units[0]] + [along_x(units[s], -s) for s in range(1, NX)]
    far_units = other_core(join_far(units))
    block = jnp.sum(blocks.astype(F32), axis=0).astype(BF)
    blocks = spread(block, context, NY * NZ)

    j6 = jnp.arange(MOST)
    token_is = (keep_pos[0][None, :] == jnp.arange(tok_dev)[:, None]) & (j6 < keep_count[0])[None, :]
    slot_of = jnp.max(jnp.where(token_is, start_here + j6[None, :], -1), axis=1)
    owner = (slot_of[:, None] == jnp.arange(KEPT)[None, :]).astype(BF)
    grad_tokens, summed = finish(blocks, owner, grad_out)
    grad_gate, grad_up, grad_down = unpack_grads(units, far_units)
    return (grad_tokens, grad_gate, grad_up, grad_down, summed)


def solution(mesh):
    grid = Mesh(mesh.devices.reshape(NY, NZ, NX, NC), ("y", "z", "x", "core"))
    context, tensor = ("y", "z"), ("x", "core")
    units = P(tensor + context, None)
    return jax.shard_map(
        body,
        mesh=grid,
        in_specs=(
            P(context, tensor),
            P(context, tensor),
            P(context),
            P(context, None),
            P(context, None),
            units,
            units,
            units,
        ),
        out_specs=(P(context, tensor), units, units, units, P(None, tensor)),
        check_vma=False,
    )
```

```python
import jax
import jax.numpy as jnp
from jax import lax
from jax.experimental import pallas as pl
from jax.experimental.pallas import tpu as pltpu
from jax.sharding import Mesh, PartitionSpec as P

NY, NZ, NX, NC = 4, 16, 4, 2
NT = NX * NC
HEAVY = 12
MOST = 6
PLANE = 35
SENT = 72
KEPT = 128
ROWS, COLS = 8, 256
BF = jnp.bfloat16
F32 = jnp.float32
VMEM = pl.BlockSpec(memory_space=pltpu.VMEM)
SMEM = pl.BlockSpec(memory_space=pltpu.SMEM)
ANY = pl.BlockSpec(memory_space=pl.ANY)
ROOM = pltpu.CompilerParams(vmem_limit_bytes=40 << 20)


def cost(flops, size):
    return pl.CostEstimate(flops=flops, bytes_accessed=size, transcendentals=0)


def dot_t(a, b):
    return lax.dot_general(a, b, (((1,), (1,)), ((), ())), preferred_element_type=F32)


def t_dot(a, b):
    return lax.dot_general(a, b, (((0,), (0,)), ((), ())), preferred_element_type=F32)


def exchange(pieces, axes):
    return lax.all_to_all(pieces, axes, 0, 0, tiled=True)


def spread(piece, axes, n):
    return exchange(jnp.broadcast_to(piece[None], (n,) + piece.shape), axes)


def along_x(array, s):
    return lax.ppermute(array, "x", [(i, (i + s) % NX) for i in range(NX)])


def other_core(array):
    return lax.ppermute(array, "core", [(0, 1), (1, 0)])


def pick_kernel(count, pos, router, tokens, grad_out, out):
    tok_dev, width = tokens.shape
    row = lax.broadcasted_iota(jnp.int32, (8, tok_dev), 0)
    lane = lax.broadcasted_iota(jnp.int32, (8, tok_dev), 1)
    at = jnp.full((8, tok_dev), -1, jnp.int32)
    weight = jnp.zeros((8, tok_dev), F32)
    for j in range(MOST):
        at = jnp.where((row == j) & (j < count[0]), pos[0, j], at)
        weight = jnp.where(row == j, router[0:1, j : j + 1].astype(F32), weight)
    picker = jnp.where(lane == at, 1.0, 0.0).astype(BF)
    meta = jnp.where(lane == 0, weight, 0.0)
    meta = jnp.where(lane == 1, 1.0, meta)
    meta = jnp.where(lane == 3, row.astype(F32), meta)
    meta = jnp.where(row < count[0], meta, 0.0)
    x = jnp.dot(picker, tokens[...], preferred_element_type=F32)
    dy = jnp.dot(picker, grad_out[...], preferred_element_type=F32)
    both = jnp.concatenate(
        [jnp.concatenate([x, meta], axis=1), jnp.concatenate([dy, meta], axis=1)], axis=0
    ).astype(BF)
    for y in range(NY):
        out[y] = both


def pick_rows(keep_count, keep_pos, router, tokens, grad_out):
    tok_dev, width = tokens.shape
    return pl.pallas_call(
        pick_kernel,
        in_specs=[SMEM, SMEM, VMEM, VMEM, VMEM],
        out_specs=VMEM,
        out_shape=jax.ShapeDtypeStruct((NY, 16, width + 128), BF),
        cost_estimate=cost(32 * tok_dev * width, 4 * tok_dev * width),
        name="pick_rows",
    )(keep_count, keep_pos, router, tokens, grad_out)


def select_kernel(column, out):
    yi, zi = lax.axis_index("y"), lax.axis_index("z")
    flat = column[...].reshape(64, column.shape[2])
    width = column.shape[2] - 128
    row = lax.broadcasted_iota(jnp.int32, (64, 128), 0)
    lane = lax.broadcasted_iota(jnp.int32, (64, 128), 1)
    shard = (row // 16 * NZ + zi).astype(F32).astype(BF)
    meta = jnp.where(lane == 2, shard, flat[:, width:])
    m = lax.broadcasted_iota(jnp.int32, (64, 8), 0)
    o = lax.broadcasted_iota(jnp.int32, (64, 8), 1)
    qy, half, qj = m // 16, m // 8 % 2, m % 8
    valid = flat[:, width + 1 : width + 2].astype(F32) > 0.5
    heavy = zi < HEAVY
    steady = jnp.where(
        heavy,
        jnp.where(qy == 0, jnp.where(qj < MOST, qj, 99), jnp.where(qj == 0, 5 + qy, 99)),
        jnp.where(qj == 0, qy, 99),
    )
    light = jnp.logical_or(qy > 0, jnp.logical_not(heavy))
    extra = jnp.where(valid & (qj >= 1) & light, 1.0, 0.0)
    r = lax.broadcasted_iota(jnp.int32, (64, 64), 0)
    c = lax.broadcasted_iota(jnp.int32, (64, 64), 1)
    before = jnp.where((c < r) & (c // 8 % 2 == r // 8 % 2), 1.0, 0.0).astype(BF)
    nth = jnp.dot(before, extra.astype(BF), preferred_element_type=F32)
    p = o % 4
    turn = lax.rem(yi - zi + NZ, NY)
    take = jnp.where(
        p < 3,
        jnp.where(steady == 4 * p + turn, 1.0, 0.0),
        jnp.where(nth == yi.astype(F32), extra, 0.0),
    )
    hot = jnp.where(half == o // 4, take, 0.0).astype(BF)
    picked = t_dot(hot, flat[:, :width]).astype(BF)
    facts = t_dot(hot, meta).astype(BF)
    for z in range(NZ):
        out[z, :, :width] = picked
        out[z, :, width:] = facts


def select_rows(column):
    return pl.pallas_call(
        select_kernel,
        in_specs=[VMEM],
        out_specs=VMEM,
        out_shape=jax.ShapeDtypeStruct((NZ, 8, column.shape[2]), BF),
        cost_estimate=cost(16 * column.size, 8 * column.size),
        name="select_rows",
    )(column)


def compact_kernel(plane, _, out):
    width = out.shape[2]
    flat = plane[...].astype(F32).reshape(128, width + 128).astype(BF)
    valid = jnp.where(flat[:, width + 1 : width + 2].astype(F32) > 0.5, 1.0, 0.0)
    r = lax.broadcasted_iota(jnp.int32, (128, 128), 0)
    c = lax.broadcasted_iota(jnp.int32, (128, 128), 1)
    before = jnp.where((c < r) & (c // 4 % 2 == r // 4 % 2), 1.0, 0.0).astype(BF)
    valid = jnp.broadcast_to(valid, (128, 128))
    rank = jnp.dot(before, valid.astype(BF), preferred_element_type=F32)
    rank = rank + jnp.where(r // 4 % 2 == 1, float(PLANE), 0.0)
    hot = jnp.where(rank == c.astype(F32), valid, 0.0).astype(BF)
    rows = t_dot(hot[:, :SENT], flat[:, :width])
    facts = t_dot(flat[:, width:], hot)
    facts = jnp.concatenate([facts[v : v + 1] for v in range(4)], axis=1)
    facts = jnp.concatenate([facts, jnp.zeros((1, width - 512), F32)], axis=1)
    row = lax.broadcasted_iota(jnp.int32, (SENT, width), 0)
    rows = jnp.where(row == 2 * PLANE, facts, rows).astype(BF)
    for y in range(NY):
        out[y] = rows


def compact_rows(plane, after):
    width = plane.shape[2] - 128
    return pl.pallas_call(
        compact_kernel,
        in_specs=[VMEM, ANY],
        out_specs=VMEM,
        out_shape=jax.ShapeDtypeStruct((NY, SENT, width), BF),
        cost_estimate=cost(256 * plane.size, 8 * plane.size),
        name="compact_rows",
    )(plane, after)


def run_copies(pairs, sems):
    copies = [
        pltpu.make_async_copy(source, target, sems.at[i])
        for i, (source, target) in enumerate(pairs)
    ]
    for copy in copies:
        copy.start()
    for copy in copies:
        copy.wait()


def peer(s, d):
    x, core = lax.axis_index("x"), lax.axis_index("core")
    return lax.rem(x + s + NX, NX) * NC + lax.rem(core + d, NC)


def features(whole, t, width):
    return whole.at[:, pl.ds(pl.multiple_of(t * width, width), width)]


def third(packed, k):
    units = packed.shape[-2] // 3
    return pl.ds(k * units, units)


def pack_kernel(gate_w, up_w, down_w, _, out0, out1, out2, out3, sems):
    width = out0.shape[2]
    pairs = []
    for s, out in enumerate((out0, out1, out2, out3)):
        for d in range(NC):
            for k, w in enumerate((gate_w, up_w, down_w)):
                pairs.append((features(w, peer(s, d), width), out.at[d, third(out, k)]))
    run_copies(pairs, sems)


def pack_weights(gate_weight, up_weight, down_weight, after):
    units, full = gate_weight.shape
    out = jax.ShapeDtypeStruct((NC, 3 * units, full // NT), BF)
    return pl.pallas_call(
        pack_kernel,
        in_specs=[ANY] * 4,
        out_specs=[VMEM] * NX,
        out_shape=[out] * NX,
        scratch_shapes=[pltpu.SemaphoreType.DMA((3 * NT,))],
        cost_estimate=cost(0, 12 * units * full),
        name="pack_weights",
    )(gate_weight, up_weight, down_weight, after)


def join_kernel(*refs):
    out = refs[-1]
    for s, part in enumerate(refs[:-1]):
        out[s] = part[0]


def join_far(parts):
    n = len(parts)
    _, units3, width = parts[0].shape
    return pl.pallas_call(
        join_kernel,
        grid=(1,),
        in_specs=[pl.BlockSpec((1, units3, width), lambda i: (1, 0, 0))] * n,
        out_specs=VMEM,
        out_shape=jax.ShapeDtypeStruct((n, units3, width), BF),
        cost_estimate=cost(0, 4 * n * units3 * width),
        name="join_far",
    )(*parts)


def unpack_kernel(in0, in1, in2, in3, far, grad_gate, grad_up, grad_down, sems):
    width = far.shape[2]
    pairs = []
    for s, near in enumerate((in0, in1, in2, in3)):
        for d, part in enumerate((near.at[0], far.at[s])):
            for k, out in enumerate((grad_gate, grad_up, grad_down)):
                pairs.append((part.at[third(near, k)], features(out, peer(s, d), width)))
    run_copies(pairs, sems)


def unpack_grads(parts, far):
    _, units3, width = far.shape
    out = jax.ShapeDtypeStruct((units3 // 3, NT * width), BF)
    return pl.pallas_call(
        unpack_kernel,
        grid=(1,),
        in_specs=[near_spec(units3, width)] * NX + [VMEM],
        out_specs=[ANY] * 3,
        out_shape=[out] * 3,
        scratch_shapes=[pltpu.SemaphoreType.DMA((3 * NT,))],
        cost_estimate=cost(0, 4 * NT * units3 * width),
        name="unpack_grads",
    )(*parts, far)


def near_spec(units3, width):
    return pl.BlockSpec((1, units3, width), lambda i: (0, 0, 0))


def blocks_of(near, far):
    for s in range(NX):
        yield s, 0, near[s][0]
        yield s, 1, far[s]


def slots_of(messages):
    lane = lax.broadcasted_iota(jnp.int32, (1, 128), 1)
    rows = []
    for y in range(NY):
        facts = messages[y][2 * PLANE : 2 * PLANE + 1, :512].astype(F32)
        key = facts[:, 256:384] * 8.0 + facts[:, 384:512]
        rows.append(jnp.where(facts[:, 128:256] > 0.5, key, 1e6))
    keys = jnp.concatenate([jnp.where(lane < PLANE, r, 1e6) for r in rows] * 2, axis=0).T
    for key in rows:
        slot = jnp.zeros((1, 128), F32)
        for y in range(NY):
            less = jnp.where(keys[:, y : y + 1] < key, 1.0, 0.0)
            slot += jnp.sum(less, axis=0, keepdims=True)
        yield jnp.where(key < 1e5, slot, -1000.0).astype(jnp.int32)


def order_rows(messages):
    lane = lax.broadcasted_iota(jnp.int32, (2 * KEPT, 128), 1)
    slot_id = lax.broadcasted_iota(jnp.int32, (2 * KEPT, 128), 0)
    slot_id = slot_id - jnp.where(lane < PLANE, 0, KEPT)
    total = jnp.zeros((2 * KEPT, messages.shape[2]), F32)
    for y, slots in enumerate(slots_of(messages)):
        hot = jnp.where(slot_id == slots, 1.0, 0.0).astype(BF)[:, :SENT]
        total += jnp.dot(hot, messages[y], preferred_element_type=F32)
    return total.astype(BF)


def forward_kernel(messages, w0, w1, w2, w3, far, pre):
    _, units3, width = far.shape
    units = units3 // 3
    ordered = order_rows(messages)
    blocks = list(blocks_of((w0, w1, w2, w3), far))
    both = jnp.concatenate([w[: 2 * units] for _, _, w in blocks], axis=0)
    both = dot_t(both, ordered[:KEPT])
    down = jnp.concatenate([w[2 * units :] for _, _, w in blocks], axis=0)
    down = dot_t(down, ordered[KEPT:])
    for i, (s, d, _) in enumerate(blocks):
        t = peer(-s, d)
        pre[t, : 2 * units] = both[2 * units * i : 2 * units * (i + 1)].astype(BF)
        pre[t, 2 * units :] = down[units * i : units * (i + 1)].astype(BF)


def forward(messages, near, far):
    _, units3, width = far.shape
    return pl.pallas_call(
        forward_kernel,
        grid=(1,),
        in_specs=[VMEM] + [near_spec(units3, width)] * NX + [VMEM],
        out_specs=VMEM,
        out_shape=jax.ShapeDtypeStruct((NT, units3, KEPT), BF),
        cost_estimate=cost(2 * NT * units3 * width * KEPT, 2 * NT * units3 * width),
        compiler_params=ROOM,
        name="forward",
    )(messages, *near, far)


def hidden_kernel(pre, row_scale, out):
    _, units3, _ = pre.shape
    units = units3 // 3
    total = jnp.sum(pre[...].astype(F32), axis=0)
    gate_pre, up_pre, back_proj = total[:units], total[units : 2 * units], total[2 * units :]
    sigmoid_gate = jax.nn.sigmoid(gate_pre)
    activated = gate_pre * sigmoid_gate
    hidden_grad = row_scale[...] * back_proj
    gate = hidden_grad * sigmoid_gate * (1.0 + gate_pre * (1.0 - sigmoid_gate)) * up_pre
    up = hidden_grad * activated
    hidden = activated * up_pre
    both = jnp.concatenate([gate, up, hidden], axis=0).astype(BF)
    for t in range(NT):
        out[t] = both


def hidden_grads(pre, row_scale):
    return pl.pallas_call(
        hidden_kernel,
        in_specs=[VMEM] * 2,
        out_specs=VMEM,
        out_shape=jax.ShapeDtypeStruct(pre.shape, BF),
        cost_estimate=cost(20 * pre.size, 6 * pre.size),
        name="hidden_grads",
    )(pre, row_scale)


def input_grad_kernel(grads, w0, w1, w2, w3, far, out):
    _, units3, width = far.shape
    units2 = units3 // 3 * 2
    blocks = list(blocks_of((w0, w1, w2, w3), far))
    g = jnp.concatenate([grads[peer(-s, d), :units2] for s, d, _ in blocks], axis=0)
    w = jnp.concatenate([w[:units2] for _, _, w in blocks], axis=0)
    total = t_dot(g, w).astype(BF)
    wide = width // COLS
    for i in range(KEPT // ROWS):
        for k in range(wide):
            out[wide * i + k] = total[ROWS * i : ROWS * (i + 1), COLS * k : COLS * (k + 1)]


def input_grad(grads, near, far):
    _, units3, width = far.shape
    pieces = KEPT // ROWS * (width // COLS)
    return pl.pallas_call(
        input_grad_kernel,
        grid=(1,),
        in_specs=[VMEM] + [near_spec(units3, width)] * NX + [VMEM],
        out_specs=VMEM,
        out_shape=jax.ShapeDtypeStruct((pieces, ROWS, COLS), BF),
        cost_estimate=cost(2 * NT * units3 * width * KEPT, 2 * NT * units3 * width),
        compiler_params=ROOM,
        name="input_grad",
    )(grads, *near, far)


def weight_grads_kernel(grads, messages, row_scale, out0, out1, out2, out3):
    _, units3, _ = out0.shape
    units = units3 // 3
    rows = order_rows(messages)
    x = rows[:KEPT]
    scaled_dy = (row_scale[...] * rows[KEPT:].astype(F32)).astype(BF)
    for s, out in enumerate((out0, out1, out2, out3)):
        for d in range(NC):
            g = grads[peer(-s, d)]
            both = jnp.dot(g[: 2 * units], x, preferred_element_type=F32)
            out[d, : 2 * units] = both.astype(BF)
            down = jnp.dot(g[2 * units :], scaled_dy, preferred_element_type=F32)
            out[d, 2 * units :] = down.astype(BF)


def weight_grads(grads, messages, row_scale):
    _, units3, _ = grads.shape
    width = messages.shape[2]
    return pl.pallas_call(
        weight_grads_kernel,
        in_specs=[VMEM] * 3,
        out_specs=[VMEM] * NX,
        out_shape=[jax.ShapeDtypeStruct((NC, units3, width), BF)] * NX,
        cost_estimate=cost(2 * NT * units3 * width * KEPT, 2 * NT * units3 * width),
        compiler_params=ROOM,
        name="weight_grads",
    )(grads, messages, row_scale)


def finish_kernel(blocks, owner, grad_out, grad_tokens, summed):
    width = grad_out.shape[1]
    wide = width // COLS
    rows = []
    for i in range(KEPT // ROWS):
        parts = [blocks[wide * i + k].astype(F32) for k in range(wide)]
        rows.append(jnp.concatenate(parts, axis=1))
    whole = jnp.concatenate(rows, axis=0)
    summed[...] = whole
    added = jnp.dot(owner[...], whole.astype(BF), preferred_element_type=F32)
    grad_tokens[...] = (grad_out[...].astype(F32) + added).astype(BF)


def finish(blocks, owner, grad_out):
    width = grad_out.shape[1]
    return pl.pallas_call(
        finish_kernel,
        in_specs=[VMEM] * 3,
        out_specs=[VMEM] * 2,
        out_shape=[
            jax.ShapeDtypeStruct(grad_out.shape, BF),
            jax.ShapeDtypeStruct((KEPT, width), F32),
        ],
        cost_estimate=cost(2 * KEPT * grad_out.size, 10 * grad_out.size),
        name="finish",
    )(blocks, owner, grad_out)


def body(tokens, grad_out, keep_count, keep_pos, router, gate_weight, up_weight, down_weight):
    tok_dev, width = tokens.shape
    yi, zi = lax.axis_index("y"), lax.axis_index("z")
    shard = yi * NZ + zi
    tensor, context = ("x", "core"), ("y", "z")

    picked = pick_rows(keep_count, keep_pos, router, tokens, grad_out)
    column = exchange(picked, "y")

    sent = pack_weights(gate_weight, up_weight, down_weight, picked)
    near = [sent[0]] + [along_x(sent[s], s) for s in range(1, NX)]
    far = other_core(join_far(near))
    plane = exchange(select_rows(column), "z")
    messages = exchange(compact_rows(plane, far), "y")

    facts = messages[:, 2 * PLANE, :512].reshape(NY, 4, 128).astype(F32)[:, :, :PLANE]
    facts = facts.transpose(1, 0, 2).reshape(4, NY * PLANE)
    valid = facts[1] > 0.5
    key = facts[2] * 8 + facts[3]
    slot = jnp.sum((key[None, :] < key[:, None]) & valid[None, :], axis=1)
    hot = (slot[None, :] == jnp.arange(KEPT)[:, None]) & valid[None, :]
    row_scale = jnp.sum(jnp.where(hot, facts[0][None, :], 0.0), axis=1)
    start_here = jnp.sum((valid & (facts[2] < shard.astype(F32))).astype(jnp.int32))

    pre = forward(messages, near, far)
    grads = hidden_grads(exchange(pre, tensor), row_scale[None, :])
    grads = exchange(grads, tensor)
    blocks = exchange(input_grad(grads, near, far), context)
    units = weight_grads(grads, messages, row_scale[:, None])
    units = [units[0]] + [along_x(units[s], -s) for s in range(1, NX)]
    far_units = other_core(join_far(units))
    block = jnp.sum(blocks.astype(F32), axis=0).astype(BF)
    blocks = spread(block, context, NY * NZ)

    j6 = jnp.arange(MOST)
    token_is = (keep_pos[0][None, :] == jnp.arange(tok_dev)[:, None]) & (j6 < keep_count[0])[None, :]
    slot_of = jnp.max(jnp.where(token_is, start_here + j6[None, :], -1), axis=1)
    owner = (slot_of[:, None] == jnp.arange(KEPT)[None, :]).astype(BF)
    grad_tokens, summed = finish(blocks, owner, grad_out)
    grad_gate, grad_up, grad_down = unpack_grads(units, far_units)
    return (grad_tokens, grad_gate, grad_up, grad_down, summed)


def solution(mesh):
    grid = Mesh(mesh.devices.reshape(NY, NZ, NX, NC), ("y", "z", "x", "core"))
    context, tensor = ("y", "z"), ("x", "core")
    units = P(tensor + context, None)
    return jax.shard_map(
        body,
        mesh=grid,
        in_specs=(
            P(context, tensor),
            P(context, tensor),
            P(context),
            P(context, None),
            P(context, None),
            units,
            units,
            units,
        ),
        out_specs=(P(context, tensor), units, units, units, P(None, tensor)),
        check_vma=False,
    )
```

```python
import jax
import jax.numpy as jnp
from jax import lax
from jax.experimental import pallas as pl
from jax.experimental.pallas import tpu as pltpu
from jax.sharding import Mesh, PartitionSpec as P

NY, NZ, NX, NC = 4, 16, 4, 2
NT = NX * NC
HEAVY = 12
MOST = 6
PLANE = 35
SENT = 72
KEPT = 128
ROWS, COLS = 8, 256
BF = jnp.bfloat16
F32 = jnp.float32
VMEM = pl.BlockSpec(memory_space=pltpu.VMEM)
SMEM = pl.BlockSpec(memory_space=pltpu.SMEM)
ANY = pl.BlockSpec(memory_space=pl.ANY)
ROOM = pltpu.CompilerParams(vmem_limit_bytes=40 << 20)


def cost(flops, size):
    return pl.CostEstimate(flops=flops, bytes_accessed=size, transcendentals=0)


def dot_t(a, b):
    return lax.dot_general(a, b, (((1,), (1,)), ((), ())), preferred_element_type=F32)


def t_dot(a, b):
    return lax.dot_general(a, b, (((0,), (0,)), ((), ())), preferred_element_type=F32)


def exchange(pieces, axes):
    return lax.all_to_all(pieces, axes, 0, 0, tiled=True)


def spread(piece, axes, n):
    return exchange(jnp.broadcast_to(piece[None], (n,) + piece.shape), axes)


def along_x(array, s):
    return lax.ppermute(array, "x", [(i, (i + s) % NX) for i in range(NX)])


def other_core(array):
    return lax.ppermute(array, "core", [(0, 1), (1, 0)])


def pick_kernel(count, pos, router, tokens, grad_out, out):
    tok_dev, width = tokens.shape
    row = lax.broadcasted_iota(jnp.int32, (8, tok_dev), 0)
    lane = lax.broadcasted_iota(jnp.int32, (8, tok_dev), 1)
    at = jnp.full((8, tok_dev), -1, jnp.int32)
    weight = jnp.zeros((8, tok_dev), F32)
    for j in range(MOST):
        at = jnp.where((row == j) & (j < count[0]), pos[0, j], at)
        weight = jnp.where(row == j, router[0:1, j : j + 1].astype(F32), weight)
    picker = jnp.where(lane == at, 1.0, 0.0).astype(BF)
    meta = jnp.where(lane == 0, weight, 0.0)
    meta = jnp.where(lane == 1, 1.0, meta)
    meta = jnp.where(lane == 3, row.astype(F32), meta)
    meta = jnp.where(row < count[0], meta, 0.0)
    x = jnp.dot(picker, tokens[...], preferred_element_type=F32)
    dy = jnp.dot(picker, grad_out[...], preferred_element_type=F32)
    both = jnp.concatenate(
        [jnp.concatenate([x, meta], axis=1), jnp.concatenate([dy, meta], axis=1)], axis=0
    ).astype(BF)
    for y in range(NY):
        out[y] = both


def pick_rows(keep_count, keep_pos, router, tokens, grad_out):
    tok_dev, width = tokens.shape
    return pl.pallas_call(
        pick_kernel,
        in_specs=[SMEM, SMEM, VMEM, VMEM, VMEM],
        out_specs=VMEM,
        out_shape=jax.ShapeDtypeStruct((NY, 16, width + 128), BF),
        cost_estimate=cost(32 * tok_dev * width, 4 * tok_dev * width),
        name="pick_rows",
    )(keep_count, keep_pos, router, tokens, grad_out)


def select_kernel(column, out):
    yi, zi = lax.axis_index("y"), lax.axis_index("z")
    flat = column[...].reshape(64, column.shape[2])
    width = column.shape[2] - 128
    row = lax.broadcasted_iota(jnp.int32, (64, 128), 0)
    lane = lax.broadcasted_iota(jnp.int32, (64, 128), 1)
    shard = (row // 16 * NZ + zi).astype(F32).astype(BF)
    meta = jnp.where(lane == 2, shard, flat[:, width:])
    m = lax.broadcasted_iota(jnp.int32, (64, 8), 0)
    o = lax.broadcasted_iota(jnp.int32, (64, 8), 1)
    qy, half, qj = m // 16, m // 8 % 2, m % 8
    valid = flat[:, width + 1 : width + 2].astype(F32) > 0.5
    heavy = zi < HEAVY
    steady = jnp.where(
        heavy,
        jnp.where(qy == 0, jnp.where(qj < MOST, qj, 99), jnp.where(qj == 0, 5 + qy, 99)),
        jnp.where(qj == 0, qy, 99),
    )
    light = jnp.logical_or(qy > 0, jnp.logical_not(heavy))
    extra = jnp.where(valid & (qj >= 1) & light, 1.0, 0.0)
    r = lax.broadcasted_iota(jnp.int32, (64, 64), 0)
    c = lax.broadcasted_iota(jnp.int32, (64, 64), 1)
    before = jnp.where((c < r) & (c // 8 % 2 == r // 8 % 2), 1.0, 0.0).astype(BF)
    nth = jnp.dot(before, extra.astype(BF), preferred_element_type=F32)
    p = o % 4
    turn = lax.rem(yi - zi + NZ, NY)
    take = jnp.where(
        p < 3,
        jnp.where(steady == 4 * p + turn, 1.0, 0.0),
        jnp.where(nth == yi.astype(F32), extra, 0.0),
    )
    hot = jnp.where(half == o // 4, take, 0.0).astype(BF)
    picked = t_dot(hot, flat[:, :width]).astype(BF)
    facts = t_dot(hot, meta).astype(BF)
    for z in range(NZ):
        out[z, :, :width] = picked
        out[z, :, width:] = facts


def select_rows(column):
    return pl.pallas_call(
        select_kernel,
        in_specs=[VMEM],
        out_specs=VMEM,
        out_shape=jax.ShapeDtypeStruct((NZ, 8, column.shape[2]), BF),
        cost_estimate=cost(16 * column.size, 8 * column.size),
        name="select_rows",
    )(column)


def compact_kernel(plane, _, out):
    width = out.shape[2]
    flat = plane[...].astype(F32).reshape(128, width + 128).astype(BF)
    valid = jnp.where(flat[:, width + 1 : width + 2].astype(F32) > 0.5, 1.0, 0.0)
    r = lax.broadcasted_iota(jnp.int32, (128, 128), 0)
    c = lax.broadcasted_iota(jnp.int32, (128, 128), 1)
    before = jnp.where((c < r) & (c // 4 % 2 == r // 4 % 2), 1.0, 0.0).astype(BF)
    valid = jnp.broadcast_to(valid, (128, 128))
    rank = jnp.dot(before, valid.astype(BF), preferred_element_type=F32)
    rank = rank + jnp.where(r // 4 % 2 == 1, float(PLANE), 0.0)
    hot = jnp.where(rank == c.astype(F32), valid, 0.0).astype(BF)
    rows = t_dot(hot[:, :SENT], flat[:, :width])
    facts = t_dot(flat[:, width:], hot)
    facts = jnp.concatenate([facts[v : v + 1] for v in range(4)], axis=1)
    facts = jnp.concatenate([facts, jnp.zeros((1, width - 512), F32)], axis=1)
    row = lax.broadcasted_iota(jnp.int32, (SENT, width), 0)
    rows = jnp.where(row == 2 * PLANE, facts, rows).astype(BF)
    for y in range(NY):
        out[y] = rows


def compact_rows(plane, after):
    width = plane.shape[2] - 128
    return pl.pallas_call(
        compact_kernel,
        in_specs=[VMEM, ANY],
        out_specs=VMEM,
        out_shape=jax.ShapeDtypeStruct((NY, SENT, width), BF),
        cost_estimate=cost(256 * plane.size, 8 * plane.size),
        name="compact_rows",
    )(plane, after)


def run_copies(pairs, sems):
    copies = [
        pltpu.make_async_copy(source, target, sems.at[i])
        for i, (source, target) in enumerate(pairs)
    ]
    for copy in copies:
        copy.start()
    for copy in copies:
        copy.wait()


def peer(s, d):
    x, core = lax.axis_index("x"), lax.axis_index("core")
    return lax.rem(x + s + NX, NX) * NC + lax.rem(core + d, NC)


def features(whole, t, width):
    return whole.at[:, pl.ds(pl.multiple_of(t * width, width), width)]


def third(packed, k):
    units = packed.shape[-2] // 3
    return pl.ds(k * units, units)


def pack_kernel(gate_w, up_w, down_w, _, out0, out1, out2, out3, sems):
    width = out0.shape[2]
    pairs = []
    for s, out in enumerate((out0, out1, out2, out3)):
        for d in range(NC):
            for k, w in enumerate((gate_w, up_w, down_w)):
                pairs.append((features(w, peer(s, d), width), out.at[d, third(out, k)]))
    run_copies(pairs, sems)


def pack_weights(gate_weight, up_weight, down_weight, after):
    units, full = gate_weight.shape
    out = jax.ShapeDtypeStruct((NC, 3 * units, full // NT), BF)
    return pl.pallas_call(
        pack_kernel,
        in_specs=[ANY] * 4,
        out_specs=[VMEM] * NX,
        out_shape=[out] * NX,
        scratch_shapes=[pltpu.SemaphoreType.DMA((3 * NT,))],
        cost_estimate=cost(0, 12 * units * full),
        name="pack_weights",
    )(gate_weight, up_weight, down_weight, after)


def join_kernel(*refs):
    out = refs[-1]
    for s, part in enumerate(refs[:-1]):
        out[s] = part[0]


def join_far(parts):
    n = len(parts)
    _, units3, width = parts[0].shape
    return pl.pallas_call(
        join_kernel,
        grid=(1,),
        in_specs=[pl.BlockSpec((1, units3, width), lambda i: (1, 0, 0))] * n,
        out_specs=VMEM,
        out_shape=jax.ShapeDtypeStruct((n, units3, width), BF),
        cost_estimate=cost(0, 4 * n * units3 * width),
        name="join_far",
    )(*parts)


def unpack_kernel(in0, in1, in2, in3, far, grad_gate, grad_up, grad_down, sems):
    width = far.shape[2]
    pairs = []
    for s, near in enumerate((in0, in1, in2, in3)):
        for d, part in enumerate((near.at[0], far.at[s])):
            for k, out in enumerate((grad_gate, grad_up, grad_down)):
                pairs.append((part.at[third(near, k)], features(out, peer(s, d), width)))
    run_copies(pairs, sems)


def unpack_grads(parts, far):
    _, units3, width = far.shape
    out = jax.ShapeDtypeStruct((units3 // 3, NT * width), BF)
    return pl.pallas_call(
        unpack_kernel,
        grid=(1,),
        in_specs=[near_spec(units3, width)] * NX + [VMEM],
        out_specs=[ANY] * 3,
        out_shape=[out] * 3,
        scratch_shapes=[pltpu.SemaphoreType.DMA((3 * NT,))],
        cost_estimate=cost(0, 4 * NT * units3 * width),
        name="unpack_grads",
    )(*parts, far)


def near_spec(units3, width):
    return pl.BlockSpec((1, units3, width), lambda i: (0, 0, 0))


def blocks_of(near, far):
    for s in range(NX):
        yield s, 0, near[s][0]
        yield s, 1, far[s]


def slots_of(messages):
    lane = lax.broadcasted_iota(jnp.int32, (1, 128), 1)
    rows = []
    for y in range(NY):
        facts = messages[y][2 * PLANE : 2 * PLANE + 1, :512].astype(F32)
        key = facts[:, 256:384] * 8.0 + facts[:, 384:512]
        rows.append(jnp.where(facts[:, 128:256] > 0.5, key, 1e6))
    keys = jnp.concatenate([jnp.where(lane < PLANE, r, 1e6) for r in rows] * 2, axis=0).T
    for key in rows:
        slot = jnp.zeros((1, 128), F32)
        for y in range(NY):
            less = jnp.where(keys[:, y : y + 1] < key, 1.0, 0.0)
            slot += jnp.sum(less, axis=0, keepdims=True)
        yield jnp.where(key < 1e5, slot, -1000.0).astype(jnp.int32)


def order_rows(messages):
    lane = lax.broadcasted_iota(jnp.int32, (2 * KEPT, 128), 1)
    slot_id = lax.broadcasted_iota(jnp.int32, (2 * KEPT, 128), 0)
    slot_id = slot_id - jnp.where(lane < PLANE, 0, KEPT)
    total = jnp.zeros((2 * KEPT, messages.shape[2]), F32)
    for y, slots in enumerate(slots_of(messages)):
        hot = jnp.where(slot_id == slots, 1.0, 0.0).astype(BF)[:, :SENT]
        total += jnp.dot(hot, messages[y], preferred_element_type=F32)
    return total.astype(BF)


def forward_kernel(messages, w0, w1, w2, w3, far, pre):
    _, units3, width = far.shape
    units = units3 // 3
    ordered = order_rows(messages)
    blocks = list(blocks_of((w0, w1, w2, w3), far))
    both = jnp.concatenate([w[: 2 * units] for _, _, w in blocks], axis=0)
    both = dot_t(both, ordered[:KEPT])
    down = jnp.concatenate([w[2 * units :] for _, _, w in blocks], axis=0)
    down = dot_t(down, ordered[KEPT:])
    for i, (s, d, _) in enumerate(blocks):
        t = peer(-s, d)
        pre[t, : 2 * units] = both[2 * units * i : 2 * units * (i + 1)].astype(BF)
        pre[t, 2 * units :] = down[units * i : units * (i + 1)].astype(BF)


def forward(messages, near, far):
    _, units3, width = far.shape
    return pl.pallas_call(
        forward_kernel,
        grid=(1,),
        in_specs=[VMEM] + [near_spec(units3, width)] * NX + [VMEM],
        out_specs=VMEM,
        out_shape=jax.ShapeDtypeStruct((NT, units3, KEPT), BF),
        cost_estimate=cost(2 * NT * units3 * width * KEPT, 2 * NT * units3 * width),
        compiler_params=ROOM,
        name="forward",
    )(messages, *near, far)


def hidden_grads(pre, row_scale):
    units = pre.shape[1] // 3
    total = jnp.sum(pre.astype(F32), axis=0)
    gate_pre, up_pre, back_proj = total[:units], total[units : 2 * units], total[2 * units :]
    sigmoid_gate = jax.nn.sigmoid(gate_pre)
    activated = gate_pre * sigmoid_gate
    hidden_grad = row_scale * back_proj
    gate = hidden_grad * sigmoid_gate * (1.0 + gate_pre * (1.0 - sigmoid_gate)) * up_pre
    both = jnp.concatenate([gate, hidden_grad * activated, activated * up_pre], axis=0)
    return jnp.broadcast_to(both.astype(BF)[None], pre.shape)


def input_grad_kernel(grads, w0, w1, w2, w3, far, out):
    _, units3, width = far.shape
    units2 = units3 // 3 * 2
    blocks = list(blocks_of((w0, w1, w2, w3), far))
    g = jnp.concatenate([grads[peer(-s, d), :units2] for s, d, _ in blocks], axis=0)
    w = jnp.concatenate([w[:units2] for _, _, w in blocks], axis=0)
    total = t_dot(g, w).astype(BF)
    wide = width // COLS
    for i in range(KEPT // ROWS):
        for k in range(wide):
            out[wide * i + k] = total[ROWS * i : ROWS * (i + 1), COLS * k : COLS * (k + 1)]


def input_grad(grads, near, far):
    _, units3, width = far.shape
    pieces = KEPT // ROWS * (width // COLS)
    return pl.pallas_call(
        input_grad_kernel,
        grid=(1,),
        in_specs=[VMEM] + [near_spec(units3, width)] * NX + [VMEM],
        out_specs=VMEM,
        out_shape=jax.ShapeDtypeStruct((pieces, ROWS, COLS), BF),
        cost_estimate=cost(2 * NT * units3 * width * KEPT, 2 * NT * units3 * width),
        compiler_params=ROOM,
        name="input_grad",
    )(grads, *near, far)


def weight_grads_kernel(grads, messages, row_scale, out0, out1, out2, out3):
    _, units3, _ = out0.shape
    units = units3 // 3
    rows = order_rows(messages)
    x = rows[:KEPT]
    scaled_dy = (row_scale[...] * rows[KEPT:].astype(F32)).astype(BF)
    for s, out in enumerate((out0, out1, out2, out3)):
        for d in range(NC):
            g = grads[peer(-s, d)]
            both = jnp.dot(g[: 2 * units], x, preferred_element_type=F32)
            out[d, : 2 * units] = both.astype(BF)
            down = jnp.dot(g[2 * units :], scaled_dy, preferred_element_type=F32)
            out[d, 2 * units :] = down.astype(BF)


def weight_grads(grads, messages, row_scale):
    _, units3, _ = grads.shape
    width = messages.shape[2]
    return pl.pallas_call(
        weight_grads_kernel,
        in_specs=[VMEM] * 3,
        out_specs=[VMEM] * NX,
        out_shape=[jax.ShapeDtypeStruct((NC, units3, width), BF)] * NX,
        cost_estimate=cost(2 * NT * units3 * width * KEPT, 2 * NT * units3 * width),
        compiler_params=ROOM,
        name="weight_grads",
    )(grads, messages, row_scale)


def finish_kernel(blocks, owner, grad_out, grad_tokens, summed):
    width = grad_out.shape[1]
    wide = width // COLS
    rows = []
    for i in range(KEPT // ROWS):
        parts = [blocks[wide * i + k].astype(F32) for k in range(wide)]
        rows.append(jnp.concatenate(parts, axis=1))
    whole = jnp.concatenate(rows, axis=0)
    summed[...] = whole
    added = jnp.dot(owner[...], whole.astype(BF), preferred_element_type=F32)
    grad_tokens[...] = (grad_out[...].astype(F32) + added).astype(BF)


def finish(blocks, owner, grad_out):
    width = grad_out.shape[1]
    return pl.pallas_call(
        finish_kernel,
        in_specs=[VMEM] * 3,
        out_specs=[VMEM] * 2,
        out_shape=[
            jax.ShapeDtypeStruct(grad_out.shape, BF),
            jax.ShapeDtypeStruct((KEPT, width), F32),
        ],
        cost_estimate=cost(2 * KEPT * grad_out.size, 10 * grad_out.size),
        name="finish",
    )(blocks, owner, grad_out)


def body(tokens, grad_out, keep_count, keep_pos, router, gate_weight, up_weight, down_weight):
    tok_dev, width = tokens.shape
    yi, zi = lax.axis_index("y"), lax.axis_index("z")
    shard = yi * NZ + zi
    tensor, context = ("x", "core"), ("y", "z")

    picked = pick_rows(keep_count, keep_pos, router, tokens, grad_out)
    column = exchange(picked, "y")

    sent = pack_weights(gate_weight, up_weight, down_weight, picked)
    near = [sent[0]] + [along_x(sent[s], s) for s in range(1, NX)]
    far = other_core(join_far(near))
    plane = exchange(select_rows(column), "z")
    messages = exchange(compact_rows(plane, far), "y")

    facts = messages[:, 2 * PLANE, :512].reshape(NY, 4, 128).astype(F32)[:, :, :PLANE]
    facts = facts.transpose(1, 0, 2).reshape(4, NY * PLANE)
    valid = facts[1] > 0.5
    key = facts[2] * 8 + facts[3]
    slot = jnp.sum((key[None, :] < key[:, None]) & valid[None, :], axis=1)
    hot = (slot[None, :] == jnp.arange(KEPT)[:, None]) & valid[None, :]
    row_scale = jnp.sum(jnp.where(hot, facts[0][None, :], 0.0), axis=1)
    start_here = jnp.sum((valid & (facts[2] < shard.astype(F32))).astype(jnp.int32))

    pre = forward(messages, near, far)
    grads = hidden_grads(exchange(pre, tensor), row_scale[None, :])
    grads = exchange(grads, tensor)
    blocks = exchange(input_grad(grads, near, far), context)
    units = weight_grads(grads, messages, row_scale[:, None])
    units = [units[0]] + [along_x(units[s], -s) for s in range(1, NX)]
    far_units = other_core(join_far(units))
    block = jnp.sum(blocks.astype(F32), axis=0).astype(BF)
    blocks = spread(block, context, NY * NZ)

    j6 = jnp.arange(MOST)
    token_is = (keep_pos[0][None, :] == jnp.arange(tok_dev)[:, None]) & (j6 < keep_count[0])[None, :]
    slot_of = jnp.max(jnp.where(token_is, start_here + j6[None, :], -1), axis=1)
    owner = (slot_of[:, None] == jnp.arange(KEPT)[None, :]).astype(BF)
    grad_tokens, summed = finish(blocks, owner, grad_out)
    grad_gate, grad_up, grad_down = unpack_grads(units, far_units)
    return (grad_tokens, grad_gate, grad_up, grad_down, summed)


def solution(mesh):
    grid = Mesh(mesh.devices.reshape(NY, NZ, NX, NC), ("y", "z", "x", "core"))
    context, tensor = ("y", "z"), ("x", "core")
    units = P(tensor + context, None)
    return jax.shard_map(
        body,
        mesh=grid,
        in_specs=(
            P(context, tensor),
            P(context, tensor),
            P(context),
            P(context, None),
            P(context, None),
            units,
            units,
            units,
        ),
        out_specs=(P(context, tensor), units, units, units, P(None, tensor)),
        check_vma=False,
    )
```
